256 devices in a mesh: frag: 32 (over z, x), band: 8 (over y, core).
Axes of the slice: x: 4, y: 4, z: 8, core: 2. Of those that a mesh axis runs over, the one named last changes fastest.
Arguments:
- wave_init: bfloat16 [32, 8, 64, 64, 128], P('frag', 'band'), may hold values from -6 to 6
- potential: float32 [1024, 256, 128], P('frag', 'band'), may hold values from -4 to 4
- fragment_order: int32 [32, 1], P('frag'), may hold values from 0 to 31, as said below
Outputs:
- density: float32 [1024, 256, 128], P('frag', 'band')
The draws below stay inside these ranges and needn't reach their ends.
Inputs may be any that keep to these rules, and one draw needn't show every extreme that they name: `fragment_order`: every group holds at least one code q with (q % 4) // 2 == 1; a group may hold the same code in two slots.
All inputs are finite; a program needn't handle non-finite values.
Results may differ from the reference program's by a relative error of at most 0.0003.
Values sent between devices are 32-bit elements; how exact they have to be, the bound alone decides.
No kernel may reach another device: no remote copies, remote signals or barrier semaphores. Data moves between devices by JAX's collectives and lax.ppermute only.
A program may use at most 64 MiB of HBM per device.

```python
import jax
import jax.numpy as jnp
from jax import lax

XC = 128
PZ = 32
PY = 32
FRAG_DEV = 1
FRAGS = 32
NB = 8
NZ = 1024
NY = 256
ZMAX = 64
YMAX = 64
N_FRAG = 32
N_BAND = 8


def draw_fragment_order(key, part):
    code_key = jax.random.fold_in(key, 11)
    slot_key = jax.random.fold_in(key, 23)
    codes = jax.random.randint(code_key, (N_FRAG, FRAG_DEV), 0, 4 * N_BAND, dtype=jnp.int32)
    chosen = jax.random.randint(slot_key, (N_FRAG,), 0, FRAG_DEV, dtype=jnp.int32)
    deepened = codes // 4 * 4 + 2 + codes % 2
    group_ids = jnp.arange(N_FRAG, dtype=jnp.int32)
    deepened = jnp.where((group_ids == 0)[:, None], 4 * N_BAND - 1, deepened)
    slot_ids = jnp.arange(FRAG_DEV, dtype=jnp.int32)
    return jnp.where(slot_ids[None, :] == chosen[:, None], deepened, codes).astype(jnp.int32)


def levels(rng, shape, shards, least, largest):
    def one(dim, parts):
        heights = jax.random.uniform(jax.random.fold_in(jax.random.fold_in(rng, 6), dim), (parts,), jnp.float32, least / len(shards), largest / len(shards))
        return jnp.repeat(jnp.exp(heights), shape[dim] // parts).reshape((-1,) + (1,) * (len(shape) - dim - 1))

    level = one(*shards[0])
    for cut in shards[1:]:
        level = level * one(*cut)
    return level


def normal_values(own_key, shape, scale, bound, shards=(), kind=jnp.bfloat16):
    result = jax.random.normal(own_key, shape, jnp.float32) * scale
    if len(shards) > 0:
        result = levels(own_key, shape, shards, -0.22, 0.18) * result
    return jnp.clip(result, min=-bound, max=bound).astype(kind)


def setup_inputs(seed: int = 0) -> dict:
    key_of = jax.random.split(jax.random.key(seed), 4)
    return {
        "wave_init": normal_values(key_of[0], (FRAGS, NB, ZMAX, YMAX, XC), 1.0, 6.0, ((0, 32), (1, 8))),
        "potential": normal_values(key_of[1], (NZ, NY, XC), 1.0, 4.0, ((0, 32), (1, 8)), jnp.float32),
        "fragment_order": draw_fragment_order(jax.random.fold_in(key_of[3], 71), 0),
    }


STEP_LENGTH = 0.1
EPSILON = 1e-06

def kinetic(extent, live_length):
    positions = jnp.arange(live_length, dtype=jnp.int32)
    angles = (positions[:, None] * positions[None, :] % live_length).astype(jnp.float32) * (2.0 * jnp.pi / live_length)
    folded = jnp.minimum(positions, live_length - positions).astype(jnp.float32)
    weight = (2.0 * jnp.pi * folded / live_length) ** 2
    cosine = jnp.cos(angles)
    sine = jnp.sin(angles)
    matrix = jnp.dot(cosine * weight[None, :], cosine.T, precision=lax.Precision.HIGHEST)
    matrix = matrix + jnp.dot(sine * weight[None, :], sine.T, precision=lax.Precision.HIGHEST)
    matrix = matrix / live_length
    return jnp.pad(matrix, ((0, extent - live_length), (0, extent - live_length)))

def geometry(slot_ids, columns, box_depth, box_width, length):
    piece_column = slot_ids // 4
    z_double = slot_ids % 4 // 2
    y_double = slot_ids % 2
    column_ids = jnp.arange(columns, dtype=jnp.int32)
    lower_pick = (piece_column[:, None] == column_ids[None, :]).astype(jnp.float32)
    upper_pick = (((piece_column + 1) % columns)[:, None] == column_ids[None, :]).astype(jnp.float32)
    z_lines = jnp.arange(box_depth, dtype=jnp.int32)
    y_lines = jnp.arange(box_width, dtype=jnp.int32)
    live_z = z_lines[None, :] < (box_depth // 2 * (1 + z_double))[:, None]
    live_y = y_lines[None, :] < (box_width // 2 * (1 + y_double))[:, None]
    live_mask = (live_z[:, :, None] & live_y[:, None, :]).astype(jnp.float32)[..., None]
    box_cells = (box_depth // 2 * (1 + z_double) * (box_width // 2) * (1 + y_double) * length).astype(jnp.float32)
    fragment_sign = jnp.where(z_double == y_double, 1.0, -1.0).astype(jnp.float32)
    z_ops = jnp.where((z_double == 1)[:, None, None], kinetic(box_depth, box_depth)[None], kinetic(box_depth, box_depth // 2)[None])
    y_ops = jnp.where((y_double == 1)[:, None, None], kinetic(box_width, box_width)[None], kinetic(box_width, box_width // 2)[None])
    return (lower_pick, upper_pick, live_mask, box_cells, fragment_sign, z_ops, y_ops)

def hamiltonian(states, box_potential, live_mask, x_op, z_ops, y_ops):
    spectral = jnp.einsum('sbzyx,xw->sbzyw', states, x_op, precision=lax.Precision.HIGHEST)
    spectral = spectral + jnp.einsum('sbzyx,szw->sbwyx', states, z_ops, precision=lax.Precision.HIGHEST)
    spectral = spectral + jnp.einsum('sbzyx,syw->sbzwx', states, y_ops, precision=lax.Precision.HIGHEST)
    applied = 0.5 * spectral + box_potential[:, None] * states
    return applied * live_mask[:, None]

def gradient_step(states, box_potential, live_mask, box_cells, x_op, z_ops, y_ops):
    applied = hamiltonian(states, box_potential, live_mask, x_op, z_ops, y_ops)
    intersection = lax.optimization_barrier(jnp.sum(states * states, axis=(2, 3, 4))) + EPSILON
    rayleigh = lax.optimization_barrier(jnp.sum(states * applied, axis=(2, 3, 4))) / intersection
    stepped = states - STEP_LENGTH * (applied - rayleigh[:, :, None, None, None] * states)
    weight = lax.optimization_barrier(jnp.sum(stepped * stepped, axis=(2, 3, 4))) + EPSILON
    return stepped * jnp.sqrt(box_cells[:, None] / weight)[:, :, None, None, None]

def reference(wave_init, potential, fragment_order):
    x_op = kinetic(XC, XC)
    doubled = jnp.concatenate([potential, potential[:2 * PZ]], axis=0)

    def group_density(group_index):
        slot_ids = lax.dynamic_index_in_dim(fragment_order, group_index, 0, keepdims=False)
        lower_pick, upper_pick, live_mask, box_cells, fragment_sign, z_ops, y_ops = geometry(slot_ids, N_BAND, ZMAX, YMAX, XC)
        region = lax.dynamic_slice_in_dim(doubled, group_index * PZ, 2 * PZ, 0)
        region_cols = region.reshape(2 * PZ, N_BAND, PY, XC)
        lower_box = jnp.einsum('sp,zpqx->szqx', lower_pick, region_cols, precision=lax.Precision.HIGHEST)
        upper_box = jnp.einsum('sp,zpqx->szqx', upper_pick, region_cols, precision=lax.Precision.HIGHEST)
        box_potential = jnp.concatenate([lower_box, upper_box], axis=2)
        states = lax.dynamic_slice_in_dim(wave_init, group_index * FRAG_DEV, FRAG_DEV, 0).astype(jnp.float32)
        states = states * live_mask[:, None]
        for repeat in range(2):
            states = gradient_step(states, box_potential, live_mask, box_cells, x_op, z_ops, y_ops)
        box_density = fragment_sign[:, None, None, None] * lax.optimization_barrier(jnp.sum(states * states, axis=1)) / NB
        placed = jnp.einsum('sp,szqx->zpqx', lower_pick, box_density[:, :, :PY], precision=lax.Precision.HIGHEST)
        placed = placed + jnp.einsum('sp,szqx->zpqx', upper_pick, box_density[:, :, PY:], precision=lax.Precision.HIGHEST)
        return placed.reshape(2 * PZ, NY, XC)
    regions = lax.map(group_density, jnp.arange(N_FRAG, dtype=jnp.int32))
    density = regions[:, :PZ] + jnp.roll(regions[:, PZ:], 1, axis=0)
    return density.reshape(NZ, NY, XC)
```

```python
import jax
import jax.numpy as jnp
import numpy as np
from jax import lax
from jax.experimental import pallas as pl
from jax.experimental.pallas import tpu as pltpu
from jax.sharding import PartitionSpec as P

STEP_LENGTH = 0.1
EPSILON = 1e-06
CHIPS = 4
VMEM = pl.BlockSpec(memory_space=pltpu.VMEM)
SMEM = pl.BlockSpec(memory_space=pltpu.SMEM)
BIG = pltpu.CompilerParams(vmem_limit_bytes=48 * 1024 * 1024)


def half_kinetic(extent, length):
    m = np.arange(length)
    weight = (2.0 * np.pi * np.minimum(m, length - m) / length) ** 2
    angle = 2.0 * np.pi * (m[:, None] * m[None, :] % length) / length
    matrix = (np.cos(angle) * weight) @ np.cos(angle).T + (np.sin(angle) * weight) @ np.sin(angle).T
    out = np.zeros((extent, extent))
    out[:length, :length] = 0.5 * matrix / length
    return out


def split_const(matrix):
    whole = jnp.asarray(matrix, jnp.float32)
    high = whole.astype(jnp.bfloat16)
    return high, (whole - high.astype(jnp.float32)).astype(jnp.bfloat16)


def operators(depth, width, length):
    x_high, x_low = split_const(half_kinetic(length, length))
    z_high, z_low = split_const(np.kron(half_kinetic(depth, depth), np.eye(8)))
    y_pair = np.stack(
        [np.kron(np.eye(4), half_kinetic(width, width // 2)), np.kron(np.eye(4), half_kinetic(width, width))]
    )
    y_high, y_low = split_const(y_pair)
    return jnp.stack([x_high, x_low]), jnp.stack([z_high, z_low]), jnp.stack([y_high, y_low])


def split(value):
    high = value.astype(jnp.bfloat16)
    return high, (value - high.astype(jnp.float32)).astype(jnp.bfloat16)


def dot(a, b):
    return jnp.dot(a, b, preferred_element_type=jnp.float32)


def xy_part(blocks, x_ref, y_ref, double, exact):
    parts = [(b.astype(jnp.bfloat16), None) if exact else split(b) for b in blocks]
    y_high, y_low = y_ref[0, double], y_ref[1, double]
    highs = jnp.concatenate([p[0] for p in parts], axis=1)
    y_out = dot(y_high, highs) + dot(y_low, highs)
    if not exact:
        y_out = y_out + dot(y_high, jnp.concatenate([p[1] for p in parts], axis=1))
    length = blocks[0].shape[1]
    result = []
    for i, (high, low) in enumerate(parts):
        if exact:
            x_out = dot(jnp.concatenate([high, high], 1), jnp.concatenate([x_ref[0], x_ref[1]], 0))
        else:
            x_out = dot(
                jnp.concatenate([high, low], 1), jnp.concatenate([x_ref[0], x_ref[0]], 0)
            ) + dot(high, x_ref[1])
        result.append(x_out + y_out[:, i * length : (i + 1) * length])
    return result


def z_part(blocks, z_ref, exact):
    both = jnp.concatenate(blocks, axis=1)
    if exact:
        high = both.astype(jnp.bfloat16)
        out = dot(z_ref[0], high) + dot(z_ref[1], high)
    else:
        high, low = split(both)
        out = dot(z_ref[0], high) + dot(z_ref[1], high) + dot(z_ref[0], low)
    length = blocks[0].shape[1]
    return out[:, :length], out[:, length:]


def first_kinetic(scalars, wave, x_ref, z_ref, y_ref, out, states):
    depth, width, length = out.shape
    double = scalars[0]
    live = lax.broadcasted_iota(jnp.int32, (1, width, length), 1) < (width // 2) * (1 + double)

    def xy(i, carry):
        z = i * 8
        s = jnp.where(live, wave[pl.ds(z, 8)].astype(jnp.float32), 0.0)
        states[pl.ds(z, 8)] = s
        rows = s.reshape(2, 4 * width, length)
        lower, upper = xy_part([rows[0], rows[1]], x_ref, y_ref, double, True)
        out[pl.ds(z, 4)] = lower.reshape(4, width, length)
        out[pl.ds(z + 4, 4)] = upper.reshape(4, width, length)
        return carry

    lax.fori_loop(0, depth // 8, xy, 0)

    def zz(i, carry):
        y = [pl.ds(pl.multiple_of(i * 16 + 8 * j, 8), 8) for j in range(2)]
        pieces = z_part([states[:, r].reshape(depth * 8, length) for r in y], z_ref, True)
        for r, piece in zip(y, pieces):
            out[:, r] = out[:, r] + piece.reshape(depth, 8, length)
        return carry

    lax.fori_loop(0, width // 16, zz, 0)


def total(vector):
    return jnp.sum(vector, axis=(0, 1), keepdims=True)


def fold(block):
    return jnp.sum(block.reshape(-1, 8, block.shape[-1]), axis=0)


def second_step(scalars, wave, kinetic, x_ref, z_ref, y_ref, *refs):
    chunks, (keep0, give0, keep1, give1), (trial, acc, pot) = refs[:16], refs[16:20], refs[20:]
    depth, width, length = kinetic.shape
    chunk, column = depth // 2 // CHIPS, width // 2
    double, chip, chip_keep, chip_give, at_keep = (scalars[i] for i in range(5))
    y_keep = pl.ds(pl.multiple_of(at_keep * column, column), column)
    y_give = pl.ds(pl.multiple_of((1 - at_keep) * column, column), column)
    live_rows = column * (1 + double)
    row_ids = lax.broadcasted_iota(jnp.int32, (column, length), 0)
    zero = jnp.zeros((8, length), jnp.float32)
    sums = (zero, zero, zero)
    for index, ref in enumerate(chunks):
        own, slab, m = index // 8 == 0, index // 4 % 2, index % 4
        owner, rows = (chip_keep, y_keep) if own else (chip_give, y_give)
        start = slab * (depth // 2) + lax.rem(chip - m - owner + 2 * CHIPS, CHIPS) * chunk
        half = at_keep if own else 1 - at_keep
        live = row_ids + half * column < live_rows

        def line(i, sums, ref=ref, rows=rows, start=start, live=live):
            z = start + i
            s = jnp.where(live, wave[z, rows].astype(jnp.float32), 0.0)
            v = ref[i]
            h = kinetic[z, rows] + v * s
            pot[z, rows] = v
            trial[z, rows] = h
            return (sums[0] + fold(s * s), sums[1] + fold(s * h), sums[2] + fold(h * h))

        sums = lax.fori_loop(0, chunk, line, sums, unroll=2)
    ss, sh, hh = (total(v) for v in sums)
    cells = (depth * column * length * (1 + double)).astype(jnp.float32)
    rayleigh = sh / (ss + EPSILON)
    shrink = 1.0 + STEP_LENGTH * rayleigh
    live_all = lax.broadcasted_iota(jnp.int32, (1, width, length), 1) < live_rows

    def xy(i, tt):
        z = i * 8
        s = jnp.where(live_all, wave[pl.ds(z, 8)].astype(jnp.float32), 0.0)
        t = shrink.reshape(1, 1, 1) * s - STEP_LENGTH * trial[pl.ds(z, 8)]
        trial[pl.ds(z, 8)] = t
        rows = t.reshape(2, 4 * width, length)
        lower, upper = xy_part([rows[0], rows[1]], x_ref, y_ref, double, False)
        acc[pl.ds(z, 4)] = lower.reshape(4, width, length)
        acc[pl.ds(z + 4, 4)] = upper.reshape(4, width, length)
        return tt + fold(t * t)

    tt = total(lax.fori_loop(0, depth // 8, xy, zero))

    def zz(i, sums):
        y = [pl.ds(pl.multiple_of(i * 16 + 8 * j, 8), 8) for j in range(2)]
        blocks = [trial[:, r].reshape(depth * 8, length) for r in y]
        pieces = z_part(blocks, z_ref, False)
        for r, t, piece in zip(y, blocks, pieces):
            h = acc[:, r].reshape(depth * 8, length) + piece + pot[:, r].reshape(depth * 8, length) * t
            acc[:, r] = h.reshape(depth, 8, length)
            sums = (sums[0] + fold(t * h), sums[1] + fold(h * h))
        return sums

    th, hh = (total(v) for v in lax.fori_loop(0, width // 16, zz, (zero, zero)))
    square = cells / (tt + EPSILON)
    rayleigh = square * th / (square * tt + EPSILON)
    shrink = 1.0 + STEP_LENGTH * rayleigh
    weight = shrink * shrink * tt - 2.0 * STEP_LENGTH * shrink * th + STEP_LENGTH * STEP_LENGTH * hh
    sign = (2 * double - 1).astype(jnp.float32)
    factor = sign / 8.0 * square * cells / (square * weight + EPSILON)
    for slab, kept, given in ((1, keep1, give1), (0, keep0, give0)):
        for k in range(CHIPS):
            for out, owner, rows in ((given, chip_give, y_give), (kept, chip_keep, y_keep)):
                start = slab * (depth // 2) + lax.rem(chip + k - owner + CHIPS, CHIPS) * chunk

                def line(i, carry, out=out, rows=rows, start=start, k=k):
                    z = start + i
                    u = shrink * trial[z, rows] - STEP_LENGTH * acc[z, rows]
                    out[k, i] = factor * (u * u)
                    return carry

                lax.fori_loop(0, chunk, line, 0, unroll=2)


def to_next_chip(block, k):
    return lax.ppermute(block, "band", [(b, (b + 2 * k) % (2 * CHIPS)) for b in range(2 * CHIPS)])


def to_other_core(block):
    return lax.ppermute(block, "band", [(b, b ^ 1) for b in range(2 * CHIPS)])


def to_group(block, distance):
    n = lax.axis_size("frag")
    return lax.ppermute(block, "frag", [(i, (i + distance) % n) for i in range(n)])


def place(code, core):
    low = code // 4
    upper = (low + core) % 2
    return (low + upper) % (2 * CHIPS) // 2, upper


def choose(index, options):
    out = options[0]
    for i, option in enumerate(options[1:], 1):
        out = jnp.where(index == i, option, out)
    return out


def body(wave_init, potential, fragment_order):
    _, _, depth, width, length = wave_init.shape
    chunk, column = depth // 2 // CHIPS, width // 2
    wave = wave_init[0, 0]
    band = lax.axis_index("band")
    chip, core = band // 2, band % 2
    code = fragment_order[0, 0]
    code_before = to_group(fragment_order, 1)[0, 0]
    double = code % 2
    chip_keep, at_keep = place(code, core)
    chip_give, _ = place(code, 1 - core)
    chip_before, _ = place(code_before, core)
    scalars = jnp.stack([double, chip, chip_keep, chip_give, at_keep]).astype(jnp.int32)

    pieces = potential.reshape(CHIPS, chunk, column, length)
    pieces = [pieces[0]] + [to_next_chip(pieces[k], k) for k in range(1, CHIPS)]
    below = to_group(choose((chip - chip_before) % CHIPS, pieces), -1)
    here = choose((chip - chip_keep) % CHIPS, pieces)
    own = [here] + [to_next_chip(here, k) for k in range(1, CHIPS)]
    own += [below] + [to_next_chip(below, k) for k in range(1, CHIPS)]
    other = [to_other_core(p) for p in own]

    x_op, z_op, y_op = operators(depth, width, length)
    box = jax.ShapeDtypeStruct((depth, width, length), jnp.float32)
    kinetic = pl.pallas_call(
        first_kinetic,
        out_shape=box,
        in_specs=[SMEM] + [VMEM] * 4,
        out_specs=VMEM,
        scratch_shapes=[pltpu.VMEM(box.shape, jnp.float32)],
        compiler_params=BIG,
        name="first_kinetic",
    )(scalars, wave, x_op, z_op, y_op)
    quarter = jax.ShapeDtypeStruct((CHIPS, chunk, column, length), jnp.float32)
    keep0, give0, keep1, give1 = pl.pallas_call(
        second_step,
        out_shape=[quarter] * 4,
        in_specs=[SMEM] + [VMEM] * 21,
        out_specs=[VMEM] * 4,
        scratch_shapes=[pltpu.VMEM(box.shape, jnp.float32)] * 3,
        compiler_params=BIG,
        name="second_step",
    )(scalars, wave, kinetic, x_op, z_op, y_op, *own, *other)

    def reduce_chip(keep, give):
        both = keep + to_other_core(give)
        result = both[0]
        for k in range(1, CHIPS):
            result = result + to_next_chip(both[k], k)
        return result

    above = to_group(reduce_chip(keep1, give1), 1)
    here = reduce_chip(keep0, give0)
    sends = []
    for k in range(CHIPS):
        target = (chip + k) % CHIPS
        sends.append(jnp.where(target == chip_keep, here, 0.0) + jnp.where(target == chip_before, above, 0.0))
    final = [sends[0]] + [to_next_chip(sends[k], k) for k in range(CHIPS - 1, 0, -1)]
    return jnp.concatenate(final, axis=0)


def solution(mesh):
    placed = (P("frag", "band", None, None, None), P("frag", "band", None), P("frag", None))
    return jax.shard_map(
        body, mesh=mesh, in_specs=placed, out_specs=P("frag", "band", None), check_vma=False
    )
```

```python
import jax
import jax.numpy as jnp
import numpy as np
from jax import lax
from jax.experimental import pallas as pl
from jax.experimental.pallas import tpu as pltpu
from jax.sharding import PartitionSpec as P

STEP_LENGTH = 0.1
EPSILON = 1e-06
CHIPS = 4
VMEM = pl.BlockSpec(memory_space=pltpu.VMEM)
ANY = pl.BlockSpec(memory_space=pl.ANY)
SMEM = pl.BlockSpec(memory_space=pltpu.SMEM)
BIG = pltpu.CompilerParams(vmem_limit_bytes=24 * 1024 * 1024)


def half_kinetic(extent, length):
    m = np.arange(length)
    weight = (2.0 * np.pi * np.minimum(m, length - m) / length) ** 2
    angle = 2.0 * np.pi * (m[:, None] * m[None, :] % length) / length
    matrix = (np.cos(angle) * weight) @ np.cos(angle).T + (np.sin(angle) * weight) @ np.sin(angle).T
    out = np.zeros((extent, extent))
    out[:length, :length] = 0.5 * matrix / length
    return out


def split_const(matrix):
    whole = jnp.asarray(matrix, jnp.float32)
    high = whole.astype(jnp.bfloat16)
    return high, (whole - high.astype(jnp.float32)).astype(jnp.bfloat16)


def operators(depth, width, length):
    x_high, x_low = split_const(half_kinetic(length, length))
    z_high, z_low = split_const(np.kron(half_kinetic(depth, depth), np.eye(8)))
    y_pair = np.stack(
        [np.kron(np.eye(4), half_kinetic(width, width // 2)), np.kron(np.eye(4), half_kinetic(width, width))]
    )
    y_high, y_low = split_const(y_pair)
    return jnp.stack([x_high, x_low]), jnp.stack([z_high, z_low]), jnp.stack([y_high, y_low])


def split(value):
    high = value.astype(jnp.bfloat16)
    return high, (value - high.astype(jnp.float32)).astype(jnp.bfloat16)


def dot(a, b):
    return jnp.dot(a, b, preferred_element_type=jnp.float32)


def xy_part(blocks, x_ref, y_ref, double, exact):
    parts = [(b.astype(jnp.bfloat16), None) if exact else split(b) for b in blocks]
    y_high, y_low = y_ref[0, double], y_ref[1, double]
    highs = jnp.concatenate([p[0] for p in parts], axis=1)
    y_out = dot(y_high, highs) + dot(y_low, highs)
    if not exact:
        y_out = y_out + dot(y_high, jnp.concatenate([p[1] for p in parts], axis=1))
    length = blocks[0].shape[1]
    result = []
    for i, (high, low) in enumerate(parts):
        if exact:
            x_out = dot(jnp.concatenate([high, high], 1), jnp.concatenate([x_ref[0], x_ref[1]], 0))
        else:
            x_out = dot(
                jnp.concatenate([high, low], 1), jnp.concatenate([x_ref[0], x_ref[0]], 0)
            ) + dot(high, x_ref[1])
        result.append(x_out + y_out[:, i * length : (i + 1) * length])
    return result


def z_part(blocks, z_ref, exact):
    both = jnp.concatenate(blocks, axis=1)
    if exact:
        high = both.astype(jnp.bfloat16)
        out = dot(z_ref[0], high) + dot(z_ref[1], high)
    else:
        high, low = split(both)
        out = dot(z_ref[0], high) + dot(z_ref[1], high) + dot(z_ref[0], low)
    length = blocks[0].shape[1]
    return out[:, :length], out[:, length:]


def first_kinetic(scalars, wave, x_ref, z_ref, y_ref, out, states):
    depth, width, length = out.shape
    double = scalars[0]
    live = lax.broadcasted_iota(jnp.int32, (1, width, length), 1) < (width // 2) * (1 + double)

    def xy(i, carry):
        z = i * 8
        s = jnp.where(live, wave[pl.ds(z, 8)].astype(jnp.float32), 0.0)
        states[pl.ds(z, 8)] = s
        rows = s.reshape(2, 4 * width, length)
        lower, upper = xy_part([rows[0], rows[1]], x_ref, y_ref, double, True)
        out[pl.ds(z, 4)] = lower.reshape(4, width, length)
        out[pl.ds(z + 4, 4)] = upper.reshape(4, width, length)
        return carry

    lax.fori_loop(0, depth // 8, xy, 0)

    def zz(i, carry):
        y = [pl.ds(pl.multiple_of(i * 16 + 8 * j, 8), 8) for j in range(2)]
        pieces = z_part([states[:, r].reshape(depth * 8, length) for r in y], z_ref, True)
        for r, piece in zip(y, pieces):
            out[:, r] = out[:, r] + piece.reshape(depth, 8, length)
        return carry

    lax.fori_loop(0, width // 16, zz, 0)


def total(vector):
    return jnp.sum(vector, axis=(0, 1), keepdims=True)


def fold(block):
    return jnp.sum(block.reshape(-1, 8, block.shape[-1]), axis=0)


def second_step(scalars, wave, kinetic, x_ref, z_ref, y_ref, *refs):
    chunks, (keep0, give0, keep1, give1), (trial, acc, pot) = refs[:16], refs[16:20], refs[20:]
    depth, width, length = kinetic.shape
    chunk, column = depth // 2 // CHIPS, width // 2
    double, chip, chip_keep, chip_give, at_keep = (scalars[i] for i in range(5))
    y_keep = pl.ds(pl.multiple_of(at_keep * column, column), column)
    y_give = pl.ds(pl.multiple_of((1 - at_keep) * column, column), column)
    live_rows = column * (1 + double)
    row_ids = lax.broadcasted_iota(jnp.int32, (column, length), 0)
    zero = jnp.zeros((8, length), jnp.float32)
    sums = (zero, zero, zero)
    for index, ref in enumerate(chunks):
        own, slab, m = index // 8 == 0, index // 4 % 2, index % 4
        owner, rows = (chip_keep, y_keep) if own else (chip_give, y_give)
        start = slab * (depth // 2) + ((chip - m - owner) & (CHIPS - 1)) * chunk
        half = at_keep if own else 1 - at_keep
        live = row_ids + half * column < live_rows

        def line(i, sums, ref=ref, rows=rows, start=start, live=live):
            z = start + i
            s = jnp.where(live, wave[z, rows].astype(jnp.float32), 0.0)
            v = ref[i]
            h = kinetic[z, rows] + v * s
            pot[z, rows] = v
            trial[z, rows] = h
            return (sums[0] + fold(s * s), sums[1] + fold(s * h), sums[2] + fold(h * h))

        sums = lax.fori_loop(0, chunk, line, sums, unroll=2)
    ss, sh, hh = (total(v) for v in sums)
    cells = (depth * column * length * (1 + double)).astype(jnp.float32)
    rayleigh = sh / (ss + EPSILON)
    shrink = 1.0 + STEP_LENGTH * rayleigh
    live_all = lax.broadcasted_iota(jnp.int32, (1, width, length), 1) < live_rows

    def xy(i, tt):
        z = i * 8
        s = jnp.where(live_all, wave[pl.ds(z, 8)].astype(jnp.float32), 0.0)
        t = shrink.reshape(1, 1, 1) * s - STEP_LENGTH * trial[pl.ds(z, 8)]
        trial[pl.ds(z, 8)] = t
        rows = t.reshape(2, 4 * width, length)
        lower, upper = xy_part([rows[0], rows[1]], x_ref, y_ref, double, False)
        acc[pl.ds(z, 4)] = lower.reshape(4, width, length)
        acc[pl.ds(z + 4, 4)] = upper.reshape(4, width, length)
        return tt + fold(t * t)

    tt = total(lax.fori_loop(0, depth // 8, xy, zero))

    def zz(i, sums):
        y = [pl.ds(pl.multiple_of(i * 16 + 8 * j, 8), 8) for j in range(2)]
        blocks = [trial[:, r].reshape(depth * 8, length) for r in y]
        pieces = z_part(blocks, z_ref, False)
        for r, t, piece in zip(y, blocks, pieces):
            h = acc[:, r].reshape(depth * 8, length) + piece + pot[:, r].reshape(depth * 8, length) * t
            acc[:, r] = h.reshape(depth, 8, length)
            sums = (sums[0] + fold(t * h), sums[1] + fold(h * h))
        return sums

    th, hh = (total(v) for v in lax.fori_loop(0, width // 16, zz, (zero, zero)))
    square = cells / (tt + EPSILON)
    rayleigh = square * th / (square * tt + EPSILON)
    shrink = 1.0 + STEP_LENGTH * rayleigh
    weight = shrink * shrink * tt - 2.0 * STEP_LENGTH * shrink * th + STEP_LENGTH * STEP_LENGTH * hh
    sign = (2 * double - 1).astype(jnp.float32)
    factor = sign / 8.0 * square * cells / (square * weight + EPSILON)
    for slab, kept, given in ((1, keep1, give1), (0, keep0, give0)):
        for k in range(CHIPS):
            for out, owner, rows in ((given, chip_give, y_give), (kept, chip_keep, y_keep)):
                start = slab * (depth // 2) + ((chip + k - owner) & (CHIPS - 1)) * chunk

                def line(i, carry, out=out, rows=rows, start=start, k=k):
                    z = start + i
                    u = shrink * trial[z, rows] - STEP_LENGTH * acc[z, rows]
                    out[k, i] = factor * (u * u)
                    return carry

                lax.fori_loop(0, chunk, line, 0, unroll=2)


def to_next_chip(block, k):
    return lax.ppermute(block, "band", [(b, (b + 2 * k) % (2 * CHIPS)) for b in range(2 * CHIPS)])


def to_other_core(block):
    return lax.ppermute(block, "band", [(b, b ^ 1) for b in range(2 * CHIPS)])


def to_group(block, distance, k=0):
    n, m = lax.axis_size("frag"), 2 * CHIPS
    route = [(i * m + b, (i + distance) % n * m + (b + 2 * k) % m) for i in range(n) for b in range(m)]
    return lax.ppermute(block, ("frag", "band"), route)


def place(code, core):
    low = code >> 2
    upper = (low + core) & 1
    return ((low + upper) & (2 * CHIPS - 1)) >> 1, upper


def pick(band, code, code_before, after, *refs):
    pieces, outs = refs[:CHIPS], refs[CHIPS:]
    chip, core = band[0] >> 1, band[0] & 1
    for out, order in zip(outs, (code_before, code)):
        owner, _ = place(order[0, 0], core)
        source = (chip - owner) & (CHIPS - 1)
        for k, piece in enumerate(pieces):

            @pl.when(source == k)
            def _(piece=piece, out=out):
                out[...] = piece[...]


def body(wave_init, potential, fragment_order):
    _, _, depth, width, length = wave_init.shape
    chunk, column = depth // 2 // CHIPS, width // 2
    wave = wave_init[0, 0]
    band = lax.axis_index("band")
    chip, core = band >> 1, band & 1
    code = fragment_order[0, 0]
    order_before = to_group(fragment_order, 1)
    double = code & 1
    chip_keep, at_keep = place(code, core)
    chip_give, _ = place(code, 1 - core)
    scalars = jnp.stack([double, chip, chip_keep, chip_give, at_keep]).astype(jnp.int32)

    pieces = potential.reshape(CHIPS, chunk, column, length)
    pieces = [pieces[0]] + [to_next_chip(pieces[k], k) for k in range(1, CHIPS)]

    x_op, z_op, y_op = operators(depth, width, length)
    box = jax.ShapeDtypeStruct((depth, width, length), jnp.float32)
    kinetic = pl.pallas_call(
        first_kinetic,
        out_shape=box,
        in_specs=[SMEM] + [VMEM] * 4,
        out_specs=VMEM,
        scratch_shapes=[pltpu.VMEM(box.shape, jnp.float32)],
        compiler_params=BIG,
        cost_estimate=pl.CostEstimate(flops=5_000_000_000, bytes_accessed=4_000_000, transcendentals=0),
        name="first_kinetic",
    )(scalars, wave, x_op, z_op, y_op)
    piece = jax.ShapeDtypeStruct((chunk, column, length), jnp.float32)
    below, here = pl.pallas_call(
        pick,
        out_shape=[piece] * 2,
        in_specs=[SMEM] * 3 + [ANY] + [VMEM] * CHIPS,
        out_specs=[VMEM] * 2,
        compiler_params=pltpu.CompilerParams(vmem_limit_bytes=4 * 1024 * 1024),
        name="pick",
    )(band[None].astype(jnp.int32), fragment_order, order_before, kinetic, *pieces)
    below = to_group(below, -1)
    own = [here] + [to_next_chip(here, k) for k in range(1, CHIPS)]
    own += [below] + [to_next_chip(below, k) for k in range(1, CHIPS)]
    other = [to_other_core(p) for p in own]
    quarter = jax.ShapeDtypeStruct((CHIPS, chunk, column, length), jnp.float32)
    keep0, give0, keep1, give1 = pl.pallas_call(
        second_step,
        out_shape=[quarter] * 4,
        in_specs=[SMEM] + [VMEM] * 21,
        out_specs=[VMEM] * 4,
        scratch_shapes=[pltpu.VMEM(box.shape, jnp.float32)] * 3,
        compiler_params=BIG,
        name="second_step",
    )(scalars, wave, kinetic, x_op, z_op, y_op, *own, *other)

    def reduce_chip(keep, give):
        both = keep + to_other_core(give)
        result = both[0]
        for k in range(1, CHIPS):
            result = result + to_next_chip(both[k], k)
        return result

    above = to_group(reduce_chip(keep1, give1), 1)
    here = reduce_chip(keep0, give0)
    chip_before, _ = place(order_before[0, 0], core)
    sends = []
    for k in range(CHIPS):
        target = (chip + k) & (CHIPS - 1)
        sends.append(jnp.where(target == chip_keep, here, 0.0) + jnp.where(target == chip_before, above, 0.0))
    final = [sends[0]] + [to_next_chip(sends[k], k) for k in range(CHIPS - 1, 0, -1)]
    return jnp.concatenate(final, axis=0)


def solution(mesh):
    placed = (P("frag", "band", None, None, None), P("frag", "band", None), P("frag", None))
    return jax.shard_map(
        body, mesh=mesh, in_specs=placed, out_specs=P("frag", "band", None), check_vma=False
    )
```

```python
import jax
import jax.numpy as jnp
import numpy as np
from jax import lax
from jax.experimental import pallas as pl
from jax.experimental.pallas import tpu as pltpu
from jax.sharding import PartitionSpec as P

STEP_LENGTH = 0.1
EPSILON = 1e-06
CHIPS = 4
ORDER = (1, 3, 2)
VMEM = pl.BlockSpec(memory_space=pltpu.VMEM)
ANY = pl.BlockSpec(memory_space=pl.ANY)
SMEM = pl.BlockSpec(memory_space=pltpu.SMEM)
MIDDLE = pltpu.CompilerParams(vmem_limit_bytes=16 * 1024 * 1024)
BIG = pltpu.CompilerParams(vmem_limit_bytes=24 * 1024 * 1024)


def half_kinetic(extent, length):
    m = np.arange(length)
    weight = (2.0 * np.pi * np.minimum(m, length - m) / length) ** 2
    angle = 2.0 * np.pi * (m[:, None] * m[None, :] % length) / length
    matrix = (np.cos(angle) * weight) @ np.cos(angle).T + (np.sin(angle) * weight) @ np.sin(angle).T
    out = np.zeros((extent, extent))
    out[:length, :length] = 0.5 * matrix / length
    return out


def split_const(matrix):
    whole = jnp.asarray(matrix, jnp.float32)
    high = whole.astype(jnp.bfloat16)
    return high, (whole - high.astype(jnp.float32)).astype(jnp.bfloat16)


def operators(depth, width, length):
    y_pair = [half_kinetic(width, width // 2), half_kinetic(width, width)]
    z_op, half = half_kinetic(depth, depth), depth // 2
    z_parts = [(z_op[:half, :half] + sign * z_op[:half, half:]) / 2 for sign in (1, -1)]
    rows = list(split_const(half_kinetic(length, length)))
    for matrix in y_pair:
        rows += [jnp.concatenate([part, part], axis=1) for part in split_const(matrix)]
    rows.append(jnp.concatenate([part for matrix in z_parts for part in split_const(matrix)], axis=1))
    return jnp.concatenate(rows, axis=0)


def split(value):
    high = value.astype(jnp.bfloat16)
    return high, (value - high.astype(jnp.float32)).astype(jnp.bfloat16)


def dot(a, b):
    return jnp.dot(a, b, preferred_element_type=jnp.float32)


def xy_part(blocks, x_ref, y_ref, exact):
    parts = [(b.astype(jnp.bfloat16), None) if exact else split(b) for b in blocks]
    y_high, y_low = y_ref[0], y_ref[1]
    highs = jnp.concatenate([p[0] for p in parts], axis=1)
    y_out = dot(y_high, highs) + dot(y_low, highs)
    if not exact:
        y_out = y_out + dot(y_high, jnp.concatenate([p[1] for p in parts], axis=1))
    length = blocks[0].shape[1]
    result = []
    for i, (high, low) in enumerate(parts):
        if exact:
            x_out = dot(high, x_ref[:length])
        else:
            x_out = dot(jnp.concatenate([high, low], 1), x_ref[...])
        result.append(x_out[:, :length] + x_out[:, length:] + y_out[:, i * length : (i + 1) * length])
    return result


def z_part(lowers, uppers, z_ref):
    def side_by_side(pieces):
        return jnp.concatenate([p.reshape(-1, p.shape[2]) for p in pieces], axis=1)

    upper = side_by_side(uppers)
    if lowers is None:
        inputs = [split(upper)] * 2
    else:
        lower = side_by_side(lowers)
        inputs = [split(lower + upper), split(lower - upper)]
    even, odd = (
        dot(z_ref[2 * i], high) + dot(z_ref[2 * i + 1], high) + dot(z_ref[2 * i], low)
        for i, (high, low) in enumerate(inputs)
    )
    return (even - odd, even + odd) if lowers is None else (even + odd, even - odd)


def tiles(i):
    return [pl.ds(pl.multiple_of(i * 16 + 8 * j, 8), 8) for j in range(2)]


def cut(out, j, length):
    return out[:, j * length : (j + 1) * length].reshape(-1, 8, length)


def total(vector):
    return jnp.sum(vector, axis=(0, 1), keepdims=True)


def fold(block):
    return jnp.sum(block.reshape(-1, 8, block.shape[-1]), axis=0)


def prepare(code, order_before, wave, consts, states, x_ref, y_ref, z_ref):
    depth, width, length = states.shape
    double = code[0, 0] & 1
    x_row = jnp.concatenate([consts[:length], consts[length : 2 * length]], axis=1)
    x_ref[...] = jnp.concatenate([x_row, x_row], axis=0)
    rows, cols = (lax.broadcasted_iota(jnp.int32, (4 * width, 4 * width), d) for d in range(2))
    for i in range(2):
        at = pl.ds(pl.multiple_of(2 * length + (2 * double + i) * width, width), width)
        square = jnp.concatenate([jnp.concatenate([consts[at]] * 2, axis=1)] * 4, axis=0)
        y_ref[i] = jnp.where(rows // width == cols // width, square, jnp.zeros_like(square))
    half = depth // 2
    z_rows = consts[2 * length + 4 * width : 2 * length + 4 * width + half]
    down = lax.broadcasted_iota(jnp.int32, (8 * half, half), 0) // 8 == lax.broadcasted_iota(jnp.int32, (8 * half, half), 1)
    tall = dot(down.astype(jnp.bfloat16), z_rows).astype(jnp.bfloat16)
    source, target = (lax.broadcasted_iota(jnp.int32, (length, 8 * half), d) for d in range(2))
    for i in range(4):
        full = dot(tall, (source == target // 8 + half * i).astype(jnp.bfloat16))
        z_ref[i] = jnp.where((rows & 7) == (cols & 7), full, 0.0).astype(jnp.bfloat16)
    live = lax.broadcasted_iota(jnp.int32, (1, width, length), 1) < (width // 2) * (1 + double)

    def masked(i, carry):
        states[pl.ds(i * 4, 4)] = jnp.where(live, wave[pl.ds(i * 4, 4)].astype(jnp.float32), 0.0)
        return carry

    lax.fori_loop(0, depth // 4, masked, 0)


def xy_pass(read, out, start, lines, x_ref, y_ref, exact):
    _, width, length = out.shape

    def step(i, carry):
        z = start + i * 8
        rows = read(z).reshape(2, 4 * width, length)
        lower, upper = xy_part([rows[0], rows[1]], x_ref, y_ref, exact)
        out[pl.ds(z, 4)] = lower.reshape(4, width, length)
        out[pl.ds(z + 4, 4)] = upper.reshape(4, width, length)
        return carry

    lax.fori_loop(0, lines // 8, step, 0)


def first_kinetic(after, states, x_ref, y_ref, z_ref, out):
    depth, width, length = out.shape
    half = depth // 2
    xy_pass(lambda z: states[pl.ds(z, 8)], out, 0, depth, x_ref, y_ref, True)

    def zz(i, carry):
        halves = [[states[pl.ds(j * half, half), r] for r in tiles(i)] for j in range(2)]
        for j, part in enumerate(z_part(*halves, z_ref)):
            for k, r in enumerate(tiles(i)):
                at = pl.ds(j * half, half)
                out[at, r] = out[at, r] + cut(part, k, length)
        return carry

    lax.fori_loop(0, width // 16, zz, 0)


def box_rows(band, code, column):
    at, _ = place(band[0] & 1, code[0, 0])
    return [pl.ds(pl.multiple_of(i * column, column), column) for i in (at, 1 - at)]


def line_loop(band, code, columns, use):
    chip = band[0] >> 1
    for ref, rows in zip(columns, box_rows(band, code, columns[0].shape[2])):
        chunk = ref.shape[1]
        for m in range(CHIPS):
            start = ((chip - m) & (CHIPS - 1)) * chunk

            def line(i, carry, ref=ref, rows=rows, m=m, start=start):
                use(rows, start + i, ref[m, i])
                return carry

            lax.fori_loop(0, chunk, line, 0, unroll=2)


def lower_half(band, code, states, kinetic, x_ref, y_ref, z_ref, own, other, pot, applied, again):
    half, width, length = pot.shape

    def use(rows, z, v):
        pot[z, rows] = v
        applied[z, rows] = kinetic[z, rows] + v * states[z, rows]

    line_loop(band, code, (own, other), use)
    xy_pass(lambda z: applied[pl.ds(z, 8)], again, 0, half, x_ref, y_ref, False)
    xy_pass(lambda z: kinetic[pl.ds(z, 8)], again, half, half, x_ref, y_ref, False)

    def zz(i, carry):
        lowers = [applied[:, r] for r in tiles(i)]
        uppers = [kinetic[pl.ds(half, half), r] for r in tiles(i)]
        for j, part in enumerate(z_part(lowers, uppers, z_ref)):
            for k, r in enumerate(tiles(i)):
                at = pl.ds(j * half, half)
                again[at, r] = again[at, r] + cut(part, k, length)
        return carry

    lax.fori_loop(0, width // 16, zz, 0)


def both_steps(band, code, states, kinetic, x_ref, y_ref, z_ref, pot, applied, again, own, other, *refs):
    (keep0, give0, keep1, give1), (pot_up, forced, applied_up, extra, twice) = refs[:4], refs[4:]
    half, width, length = pot.shape
    chunk, column, double = half // CHIPS, width // 2, code[0, 0] & 1

    def use(rows, z, v):
        change = v * states[half + z, rows]
        pot_up[z, rows] = v
        forced[z, rows] = change
        applied_up[z, rows] = kinetic[half + z, rows] + change

    line_loop(band, code, (own, other), use)
    xy_pass(lambda z: forced[pl.ds(z, 8)], extra, 0, half, x_ref, y_ref, False)

    def zz(i, sums):
        low_part, high_part = z_part(None, [forced[:, r] for r in tiles(i)], z_ref)
        for k, r in enumerate(tiles(i)):
            low, high = pl.ds(0, half), pl.ds(half, half)
            h, h_up = applied[:, r], applied_up[:, r]
            w = again[low, r] + cut(low_part, k, length) + pot[:, r] * h
            w_up = again[high, r] + extra[:, r] + cut(high_part, k, length) + pot_up[:, r] * h_up
            twice[low, r] = w
            twice[high, r] = w_up
            pairs = []
            for s, h, w in ((states[low, r], h, w), (states[high, r], h_up, w_up)):
                pairs.append((s * s, s * h, h * h, s * w, h * w, w * w))
            sums = tuple(v + fold(a + b) for v, a, b in zip(sums, *pairs))
        return sums

    zero = jnp.zeros((8, length), jnp.float32)
    ss, sh, hh, sw, hw, ww = (total(v) for v in lax.fori_loop(0, width // 16, zz, (zero,) * 6))
    cells = (2 * half * column * length * (1 + double)).astype(jnp.float32)
    first = 1.0 + STEP_LENGTH * sh / (ss + EPSILON)
    tt = first * first * ss - 2.0 * STEP_LENGTH * first * sh + STEP_LENGTH * STEP_LENGTH * hh
    th = first * first * sh - STEP_LENGTH * first * (hh + sw) + STEP_LENGTH * STEP_LENGTH * hw
    hh = first * first * hh - 2.0 * STEP_LENGTH * first * hw + STEP_LENGTH * STEP_LENGTH * ww
    square = cells / (tt + EPSILON)
    second = 1.0 + STEP_LENGTH * square * th / (square * tt + EPSILON)
    weight = second * second * tt - 2.0 * STEP_LENGTH * second * th + STEP_LENGTH * STEP_LENGTH * hh
    sign = (2 * double - 1).astype(jnp.float32)
    factor = sign / 8.0 * square * cells / (square * weight + EPSILON)
    by_s, by_h, by_w = second * first, -STEP_LENGTH * (first + second), STEP_LENGTH * STEP_LENGTH
    for slab, outs, source in ((1, (keep1, give1), applied_up), (0, (keep0, give0), applied)):
        for out, rows in zip(outs, box_rows(band, code, column)):
            for k in range(CHIPS):
                start = (((band[0] >> 1) + k) & (CHIPS - 1)) * chunk

                def line(i, carry, out=out, rows=rows, start=start, k=k, slab=slab, source=source):
                    z = start + i
                    at = slab * half + z
                    u = by_s * states[at, rows] + by_h * source[z, rows] + by_w * twice[at, rows]
                    out[k, i] = factor * (u * u)
                    return carry

                lax.fori_loop(0, chunk, line, 0, unroll=2)


def stack(after, *refs):
    for i, block in enumerate(refs[:-1]):
        refs[-1][i] = block[...]


def to_next_chip(block, k):
    m = 2 * CHIPS
    return lax.ppermute(block, "band", [(b, (b + 2 * k) % m) for b in range(m)])


def exchange(blocks):
    cores = [[2 * chip + core for chip in range(CHIPS)] for core in range(2)]
    return lax.all_to_all(blocks, "band", 0, 0, axis_index_groups=cores)


def around(blocks):
    sent = {k: to_next_chip(blocks[k], k) for k in ORDER}
    return [blocks[0]] + [sent[k] for k in range(1, CHIPS)]


def to_other_core(block):
    return lax.ppermute(block, "band", [(b, b ^ 1) for b in range(2 * CHIPS)])


def to_group(block, distance):
    n = lax.axis_size("frag")
    return lax.ppermute(block, "frag", [(i, (i + distance) % n) for i in range(n)])


def place(core, code):
    low = code >> 2
    upper = (low + core) & 1
    return upper, ((low + upper) & (2 * CHIPS - 1)) >> 1


def pick(band, code, code_before, after, pieces, below, here):
    for out, order in ((below, code_before), (here, code)):
        _, owner = place(band[0] & 1, order[0, 0])
        out[...] = pieces[owner]


def settle(band, *refs):
    for k, block in enumerate(refs[:CHIPS]):
        chip = ((band[0] >> 1) - k) & (CHIPS - 1)
        refs[CHIPS][pl.ds(chip * block.shape[0], block.shape[0])] = block[...]


def body(wave_init, potential, fragment_order):
    _, _, depth, width, length = wave_init.shape
    chunk, column = depth // 2 // CHIPS, width // 2
    wave = wave_init[0, 0]
    band = lax.axis_index("band").astype(jnp.int32)
    core = band & 1
    order_before = to_group(fragment_order, 1)
    pieces = exchange(potential.reshape(CHIPS, chunk, column, length))

    small = pltpu.CompilerParams(vmem_limit_bytes=4 * 1024 * 1024)
    piece, quarter, half_box, box = (
        jax.ShapeDtypeStruct(shape + (length,), jnp.float32)
        for shape in ((chunk, column), (CHIPS, chunk, column), (depth // 2, width), (depth, width))
    )
    square = (4 * width, 4 * width)
    ops = [jax.ShapeDtypeStruct(lead + square, jnp.bfloat16) for lead in ((), (2,), (4,))]

    def kernel(function, outs, spaces, params, scratch=(), flops=0):
        return pl.pallas_call(
            function,
            out_shape=outs,
            in_specs=spaces,
            out_specs=[VMEM] * len(outs),
            scratch_shapes=[pltpu.VMEM(a.shape, a.dtype) for a in scratch],
            compiler_params=params,
            cost_estimate=pl.CostEstimate(flops=flops, bytes_accessed=4_000_000, transcendentals=0) if flops else None,
            name=function.__name__,
        )

    states, *ops = kernel(prepare, [box] + ops, [SMEM, ANY, VMEM, VMEM], MIDDLE)(
        fragment_order, order_before, wave, operators(depth, width, length)
    )
    below, here = kernel(pick, [piece] * 2, [SMEM] * 3 + [ANY, VMEM], small)(
        band[None], fragment_order, order_before, states, pieces
    )
    below = to_group(below, -1)
    lower, upper = around([here] * CHIPS), around([below] * CHIPS)
    (kinetic,) = kernel(first_kinetic, [box], [ANY] + [VMEM] * 4, MIDDLE, flops=3_000_000_000)(below, states, *ops)

    def two_columns(after, blocks):
        (own,) = kernel(stack, [quarter], [ANY] + [VMEM] * CHIPS, small)(after, *blocks)
        return own, to_other_core(own)

    pot, applied, again = kernel(
        lower_half, [half_box] * 2 + [box], [SMEM] * 2 + [VMEM] * 7, MIDDLE, flops=4_000_000_000
    )(band[None], fragment_order, states, kinetic, *ops, *two_columns(kinetic, lower))
    keep0, give0, keep1, give1 = kernel(
        both_steps, [quarter] * 4, [SMEM] * 2 + [VMEM] * 10, BIG, scratch=[half_box] * 4 + [box]
    )(band[None], fragment_order, states, kinetic, *ops, pot, applied, again, *two_columns(again, upper))

    def reduce_chip(keep, give):
        result, *arrived = around(list(keep + to_other_core(give)))
        for block in arrived:
            result = result + block
        return result

    above = to_group(reduce_chip(keep1, give1), 1)
    here = reduce_chip(keep0, give0)
    owner, owner_before = (place(core, code[0, 0])[1] for code in (fragment_order, order_before))
    sends = []
    for k in range(CHIPS):
        target = ((band >> 1) + k) & (CHIPS - 1)
        sends.append(jnp.where(target == owner, here, 0.0) + jnp.where(target == owner_before, above, 0.0))
    return pl.pallas_call(
        settle,
        out_shape=jax.ShapeDtypeStruct(potential.shape, jnp.float32),
        in_specs=[SMEM] + [VMEM] * CHIPS,
        out_specs=VMEM,
        compiler_params=small,
        name="settle",
    )(band[None], *around(sends))


def solution(mesh):
    placed = (P("frag", "band", None, None, None), P("frag", "band", None), P("frag", None))
    return jax.shard_map(
        body, mesh=mesh, in_specs=placed, out_specs=P("frag", "band", None), check_vma=False
    )
```

```python
import jax
import jax.numpy as jnp
import numpy as np
from jax import lax
from jax.experimental import pallas as pl
from jax.experimental.pallas import tpu as pltpu
from jax.sharding import PartitionSpec as P

STEP_LENGTH = 0.1
EPSILON = 1e-06
CHIPS = 4
ORDER = (1, 3, 2)
VMEM = pl.BlockSpec(memory_space=pltpu.VMEM)
ANY = pl.BlockSpec(memory_space=pl.ANY)
SMEM = pl.BlockSpec(memory_space=pltpu.SMEM)
MIDDLE = pltpu.CompilerParams(vmem_limit_bytes=16 * 1024 * 1024)
BIG = pltpu.CompilerParams(vmem_limit_bytes=24 * 1024 * 1024)


def half_kinetic(extent, length):
    m = np.arange(length)
    weight = (2.0 * np.pi * np.minimum(m, length - m) / length) ** 2
    angle = 2.0 * np.pi * (m[:, None] * m[None, :] % length) / length
    matrix = (np.cos(angle) * weight) @ np.cos(angle).T + (np.sin(angle) * weight) @ np.sin(angle).T
    out = np.zeros((extent, extent))
    out[:length, :length] = 0.5 * matrix / length
    return out


def split_const(matrix):
    whole = jnp.asarray(matrix, jnp.float32)
    high = whole.astype(jnp.bfloat16)
    return high, (whole - high.astype(jnp.float32)).astype(jnp.bfloat16)


def operators(depth, width, length):
    y_pair = [half_kinetic(width, width // 2), half_kinetic(width, width)]
    z_op, half = half_kinetic(depth, depth), depth // 2
    z_parts = [(z_op[:half, :half] + sign * z_op[:half, half:]) / 2 for sign in (1, -1)]
    rows = list(split_const(half_kinetic(length, length)))
    for matrix in y_pair:
        rows += [jnp.concatenate([part, part], axis=1) for part in split_const(matrix)]
    rows.append(jnp.concatenate([part for matrix in z_parts for part in split_const(matrix)], axis=1))
    return jnp.concatenate(rows, axis=0)


def split(value):
    high = value.astype(jnp.bfloat16)
    return high, (value - high.astype(jnp.float32)).astype(jnp.bfloat16)


def dot(a, b):
    return jnp.dot(a, b, preferred_element_type=jnp.float32)


def xy_part(blocks, x_ref, y_ref, exact):
    parts = [(b.astype(jnp.bfloat16), None) if exact else split(b) for b in blocks]
    y_high, y_low = y_ref[0], y_ref[1]
    highs = jnp.concatenate([p[0] for p in parts], axis=1)
    y_out = dot(y_high, highs) + dot(y_low, highs)
    if not exact:
        y_out = y_out + dot(y_high, jnp.concatenate([p[1] for p in parts], axis=1))
    length = blocks[0].shape[1]
    result = []
    for i, (high, low) in enumerate(parts):
        if exact:
            x_out = dot(high, x_ref[:length])
        else:
            x_out = dot(jnp.concatenate([high, low], 1), x_ref[...])
        result.append(x_out[:, :length] + x_out[:, length:] + y_out[:, i * length : (i + 1) * length])
    return result


def z_part(lowers, uppers, z_ref):
    def side_by_side(pieces):
        return jnp.concatenate([p.reshape(-1, p.shape[2]) for p in pieces], axis=1)

    lower, upper = side_by_side(lowers), side_by_side(uppers)
    inputs = [split(lower + upper), split(lower - upper)]
    even, odd = (
        dot(z_ref[2 * i], high) + dot(z_ref[2 * i + 1], high) + dot(z_ref[2 * i], low)
        for i, (high, low) in enumerate(inputs)
    )
    return even + odd, even - odd


def tiles(i):
    return [pl.ds(pl.multiple_of(i * 16 + 8 * j, 8), 8) for j in range(2)]


def cut(out, j, length):
    return out[:, j * length : (j + 1) * length].reshape(-1, 8, length)


def total(vector):
    return jnp.sum(vector, axis=(0, 1), keepdims=True)


def fold(block):
    return jnp.sum(block.reshape(-1, 8, block.shape[-1]), axis=0)


def prepare(code, wave, consts, states, partly, x_ref, y_ref, z_ref):
    depth, width, length = states.shape
    double = code[0, 0] & 1
    x_row = jnp.concatenate([consts[:length], consts[length : 2 * length]], axis=1)
    x_ref[...] = jnp.concatenate([x_row, x_row], axis=0)
    rows, cols = (lax.broadcasted_iota(jnp.int32, (4 * width, 4 * width), d) for d in range(2))
    for i in range(2):
        at = pl.ds(pl.multiple_of(2 * length + (2 * double + i) * width, width), width)
        square = jnp.concatenate([jnp.concatenate([consts[at]] * 2, axis=1)] * 4, axis=0)
        y_ref[i] = jnp.where(rows // width == cols // width, square, jnp.zeros_like(square))
    half = depth // 2
    z_rows = consts[2 * length + 4 * width : 2 * length + 4 * width + half]
    down = lax.broadcasted_iota(jnp.int32, (8 * half, half), 0) // 8 == lax.broadcasted_iota(jnp.int32, (8 * half, half), 1)
    tall = dot(down.astype(jnp.bfloat16), z_rows).astype(jnp.bfloat16)
    source, target = (lax.broadcasted_iota(jnp.int32, (length, 8 * half), d) for d in range(2))
    for i in range(4):
        full = dot(tall, (source == target // 8 + half * i).astype(jnp.bfloat16))
        z_ref[i] = jnp.where((rows & 7) == (cols & 7), full, 0.0).astype(jnp.bfloat16)
    live = lax.broadcasted_iota(jnp.int32, (1, width, length), 1) < (width // 2) * (1 + double)

    def masked(z):
        s = jnp.where(live, wave[pl.ds(z, 8)].astype(jnp.float32), 0.0)
        states[pl.ds(z, 8)] = s
        return s

    xy_pass(masked, partly, 0, depth, x_ref, y_ref, True)


def xy_pass(read, out, start, lines, x_ref, y_ref, exact):
    _, width, length = out.shape

    def step(i, carry):
        z = start + i * 8
        rows = read(z).reshape(2, 4 * width, length)
        lower, upper = xy_part([rows[0], rows[1]], x_ref, y_ref, exact)
        out[pl.ds(z, 4)] = lower.reshape(4, width, length)
        out[pl.ds(z + 4, 4)] = upper.reshape(4, width, length)
        return carry

    lax.fori_loop(0, lines // 8, step, 0)


def kinetics(after, states, partly, x_ref, y_ref, z_ref, once, again):
    depth, width, length = once.shape
    half = depth // 2

    def z_pass(source, before, out):
        def zz(i, carry):
            halves = [[source[pl.ds(j * half, half), r] for r in tiles(i)] for j in range(2)]
            for j, part in enumerate(z_part(*halves, z_ref)):
                for k, r in enumerate(tiles(i)):
                    at = pl.ds(j * half, half)
                    out[at, r] = before[at, r] + cut(part, k, length)
            return carry

        lax.fori_loop(0, width // 16, zz, 0)

    z_pass(states, partly, once)
    xy_pass(lambda z: once[pl.ds(z, 8)], again, 0, depth, x_ref, y_ref, False)
    z_pass(once, again, again)


def box_rows(band, code, column):
    at, _ = place(band[0] & 1, code[0, 0])
    return [pl.ds(pl.multiple_of(i * column, column), column) for i in (at, 1 - at)]


CHUNKS = ((0, 0), (0, 1), (0, 3), (1, 0), (1, 1), (1, 3), (0, 2), (1, 2))


def line_loop(band, code, columns, half, use):
    chip = band[0] >> 1
    for ref, rows in zip(columns, box_rows(band, code, columns[0].shape[2])):
        chunk = ref.shape[1]
        for m, (slab, back) in enumerate(CHUNKS):
            start = slab * half + ((chip - back) & (CHIPS - 1)) * chunk

            def line(i, carry, ref=ref, rows=rows, m=m, start=start):
                use(rows, start + i, ref[m, i])
                return carry

            lax.fori_loop(0, chunk, line, 0, unroll=2)


def both_steps(band, code, states, kinetic, again, x_ref, y_ref, z_ref, own, other, *refs):
    (keep0, give0, keep1, give1), (pot, forced, total_h, extra, twice) = refs[:4], refs[4:]
    depth, width, length = pot.shape
    half, column, double = depth // 2, width // 2, code[0, 0] & 1
    chunk = half // CHIPS

    def use(rows, z, v):
        pot[z, rows] = v
        forced[z, rows] = v * states[z, rows]

    line_loop(band, code, (own, other), half, use)
    xy_pass(lambda z: forced[pl.ds(z, 8)], extra, 0, depth, x_ref, y_ref, False)

    def zz(i, sums):
        places = [pl.ds(0, half), pl.ds(half, half)]
        parts = z_part(*[[forced[at, r] for r in tiles(i)] for at in places], z_ref)
        for k, r in enumerate(tiles(i)):
            pairs = []
            for at, part in zip(places, parts):
                s, h = states[at, r], kinetic[at, r] + forced[at, r]
                w = again[at, r] + extra[at, r] + cut(part, k, length) + pot[at, r] * h
                total_h[at, r] = h
                twice[at, r] = w
                pairs.append((s * s, s * h, h * h, s * w, h * w, w * w))
            sums = tuple(v + fold(a + b) for v, a, b in zip(sums, *pairs))
        return sums

    zero = jnp.zeros((8, length), jnp.float32)
    ss, sh, hh, sw, hw, ww = (total(v) for v in lax.fori_loop(0, width // 16, zz, (zero,) * 6))
    cells = (2 * half * column * length * (1 + double)).astype(jnp.float32)
    first = 1.0 + STEP_LENGTH * sh / (ss + EPSILON)
    tt = first * first * ss - 2.0 * STEP_LENGTH * first * sh + STEP_LENGTH * STEP_LENGTH * hh
    th = first * first * sh - STEP_LENGTH * first * (hh + sw) + STEP_LENGTH * STEP_LENGTH * hw
    hh = first * first * hh - 2.0 * STEP_LENGTH * first * hw + STEP_LENGTH * STEP_LENGTH * ww
    square = cells / (tt + EPSILON)
    second = 1.0 + STEP_LENGTH * square * th / (square * tt + EPSILON)
    weight = second * second * tt - 2.0 * STEP_LENGTH * second * th + STEP_LENGTH * STEP_LENGTH * hh
    sign = (2 * double - 1).astype(jnp.float32)
    factor = sign / 8.0 * square * cells / (square * weight + EPSILON)
    by_s, by_h, by_w = second * first, -STEP_LENGTH * (first + second), STEP_LENGTH * STEP_LENGTH
    for slab, outs in ((1, (keep1, give1)), (0, (keep0, give0))):
        for out, rows in zip(outs, box_rows(band, code, column)):
            for k in range(CHIPS):
                start = (((band[0] >> 1) + k) & (CHIPS - 1)) * chunk

                def line(i, carry, out=out, rows=rows, start=start, k=k, slab=slab):
                    at = slab * half + start + i
                    u = by_s * states[at, rows] + by_h * total_h[at, rows] + by_w * twice[at, rows]
                    out[k, i] = factor * (u * u)
                    return carry

                lax.fori_loop(0, chunk, line, 0, unroll=2)


def stack(after, *refs):
    out, at = refs[-1], 0
    for block in refs[:-1]:
        parts = [block[...]] if len(block.shape) < len(out.shape) else [block[i] for i in range(block.shape[0])]
        for part in parts:
            out[at] = part
            at += 1


def to_next_chip(block, k):
    m = 2 * CHIPS
    return lax.ppermute(block, "band", [(b, (b + 2 * k) % m) for b in range(m)])


def around(blocks):
    sent = {k: to_next_chip(blocks[k], k) for k in ORDER}
    return [blocks[0]] + [sent[k] for k in range(1, CHIPS)]


def to_other_core(block):
    return lax.ppermute(block, "band", [(b, b ^ 1) for b in range(2 * CHIPS)])


def to_group(block, distance):
    n = lax.axis_size("frag")
    return lax.ppermute(block, "frag", [(i, (i + distance) % n) for i in range(n)])


def place(core, code):
    low = code >> 2
    upper = (low + core) & 1
    return upper, ((low + upper) & (2 * CHIPS - 1)) >> 1


def cut_chunks(band, potential, *outs):
    for k, out in enumerate(outs):
        at = (((band[0] >> 1) + k) & (CHIPS - 1)) * out.shape[0]
        out[...] = potential[pl.ds(at, out.shape[0])]


def pick(band, code, code_before, after, *refs):
    for out, order in zip(refs[CHIPS:], (code_before, code)):
        _, owner = place(band[0] & 1, order[0, 0])
        source = ((band[0] >> 1) - owner) & (CHIPS - 1)
        for k in range(CHIPS):

            @pl.when(source == k)
            def _(k=k, out=out):
                out[...] = refs[k][...]


def settle(band, *refs):
    for k, block in enumerate(refs[:CHIPS]):
        chip = ((band[0] >> 1) - k) & (CHIPS - 1)
        refs[CHIPS][pl.ds(chip * block.shape[0], block.shape[0])] = block[...]


def body(wave_init, potential, fragment_order):
    _, _, depth, width, length = wave_init.shape
    chunk, column = depth // 2 // CHIPS, width // 2
    wave = wave_init[0, 0]
    band = lax.axis_index("band").astype(jnp.int32)
    core = band & 1
    order_before = to_group(fragment_order, 1)

    small = pltpu.CompilerParams(vmem_limit_bytes=4 * 1024 * 1024)
    piece, quarter, box = (
        jax.ShapeDtypeStruct(shape + (length,), jnp.float32)
        for shape in ((chunk, column), (CHIPS, chunk, column), (depth, width))
    )
    square = (4 * width, 4 * width)
    ops = [jax.ShapeDtypeStruct(lead + square, jnp.bfloat16) for lead in ((), (2,), (4,))]

    def kernel(function, outs, spaces, params, scratch=(), flops=0):
        return pl.pallas_call(
            function,
            out_shape=outs,
            in_specs=spaces,
            out_specs=[VMEM] * len(outs),
            scratch_shapes=[pltpu.VMEM(a.shape, a.dtype) for a in scratch],
            compiler_params=params,
            cost_estimate=pl.CostEstimate(flops=flops, bytes_accessed=4_000_000, transcendentals=0) if flops else None,
            name=function.__name__,
        )

    pieces = around(kernel(cut_chunks, [piece] * CHIPS, [SMEM, VMEM], small)(band[None], potential))
    states, partly, *ops = kernel(prepare, [box] * 2 + ops, [SMEM, VMEM, VMEM], MIDDLE)(
        fragment_order, wave, operators(depth, width, length)
    )
    below, here = kernel(pick, [piece] * 2, [SMEM] * 3 + [ANY] + [VMEM] * CHIPS, small)(
        band[None], fragment_order, order_before, states, *pieces
    )
    below = to_group(below, -1)

    def stacked(after, *blocks):
        count = sum(1 if block.ndim == 3 else block.shape[0] for block in blocks)
        out = jax.ShapeDtypeStruct((count, chunk, column, length), jnp.float32)
        return kernel(stack, [out], [ANY] + [VMEM] * len(blocks), small)(after, *blocks)[0]

    near = [here] + [to_next_chip(here, k) for k in (1, 3)]
    both = stacked(states, here, below)
    far = [below] + [to_next_chip(below, k) for k in (1, 3)] + [to_next_chip(both, 2)]
    kinetic, again = kernel(kinetics, [box] * 2, [ANY] + [VMEM] * 5, MIDDLE, flops=4_000_000_000)(
        both, states, partly, *ops
    )
    own = stacked(again, *near, *far)
    keep0, give0, keep1, give1 = kernel(
        both_steps, [quarter] * 4, [SMEM] * 2 + [VMEM] * 8, BIG, scratch=[box] * 5
    )(band[None], fragment_order, states, kinetic, again, *ops, own, to_other_core(own))

    def reduce_chip(keep, give):
        result, *arrived = around(list(keep + to_other_core(give)))
        for block in arrived:
            result = result + block
        return result

    above = to_group(reduce_chip(keep1, give1), 1)
    here = reduce_chip(keep0, give0)
    owner, owner_before = (place(core, code[0, 0])[1] for code in (fragment_order, order_before))
    sends = []
    for k in range(CHIPS):
        target = ((band >> 1) + k) & (CHIPS - 1)
        sends.append(jnp.where(target == owner, here, 0.0) + jnp.where(target == owner_before, above, 0.0))
    return pl.pallas_call(
        settle,
        out_shape=jax.ShapeDtypeStruct(potential.shape, jnp.float32),
        in_specs=[SMEM] + [VMEM] * CHIPS,
        out_specs=VMEM,
        compiler_params=small,
        name="settle",
    )(band[None], *around(sends))


def solution(mesh):
    placed = (P("frag", "band", None, None, None), P("frag", "band", None), P("frag", None))
    return jax.shard_map(
        body, mesh=mesh, in_specs=placed, out_specs=P("frag", "band", None), check_vma=False
    )
```

```python
import jax
import jax.numpy as jnp
import numpy as np
from jax import lax
from jax.experimental import pallas as pl
from jax.experimental.pallas import tpu as pltpu
from jax.sharding import PartitionSpec as P

STEP_LENGTH = 0.1
EPSILON = 1e-06
CHIPS = 4
ORDER = (1, 3, 2)
VMEM = pl.BlockSpec(memory_space=pltpu.VMEM)
ANY = pl.BlockSpec(memory_space=pl.ANY)
SMEM = pl.BlockSpec(memory_space=pltpu.SMEM)
MIDDLE = pltpu.CompilerParams(vmem_limit_bytes=16 * 1024 * 1024)
BIG = pltpu.CompilerParams(vmem_limit_bytes=24 * 1024 * 1024)


def half_kinetic(extent, length):
    m = np.arange(length)
    weight = (2.0 * np.pi * np.minimum(m, length - m) / length) ** 2
    angle = 2.0 * np.pi * (m[:, None] * m[None, :] % length) / length
    matrix = (np.cos(angle) * weight) @ np.cos(angle).T + (np.sin(angle) * weight) @ np.sin(angle).T
    out = np.zeros((extent, extent))
    out[:length, :length] = 0.5 * matrix / length
    return out


def split_const(matrix):
    whole = jnp.asarray(matrix, jnp.float32)
    high = whole.astype(jnp.bfloat16)
    return high, (whole - high.astype(jnp.float32)).astype(jnp.bfloat16)


def operators(depth, width, length):
    y_pair = [half_kinetic(width, width // 2), half_kinetic(width, width)]
    z_op, half = half_kinetic(depth, depth), depth // 2
    z_parts = [(z_op[:half, :half] + sign * z_op[:half, half:]) / 2 for sign in (1, -1)]
    rows = list(split_const(half_kinetic(length, length)))
    for matrix in y_pair:
        rows += [jnp.concatenate([part, part], axis=1) for part in split_const(matrix)]
    rows.append(jnp.concatenate([part for matrix in z_parts for part in split_const(matrix)], axis=1))
    return jnp.concatenate(rows, axis=0)


def split(value):
    high = value.astype(jnp.bfloat16)
    return high, (value - high.astype(jnp.float32)).astype(jnp.bfloat16)


def dot(a, b):
    return jnp.dot(a, b, preferred_element_type=jnp.float32)


def xy_part(blocks, x_ref, y_ref, exact):
    parts = [(b.astype(jnp.bfloat16), None) if exact else split(b) for b in blocks]
    y_high, y_low = y_ref[0], y_ref[1]
    highs = jnp.concatenate([p[0] for p in parts], axis=1)
    y_out = dot(y_high, highs) + dot(y_low, highs)
    if not exact:
        y_out = y_out + dot(y_high, jnp.concatenate([p[1] for p in parts], axis=1))
    length = blocks[0].shape[1]
    result = []
    for i, (high, low) in enumerate(parts):
        if exact:
            x_out = dot(high, x_ref[:length])
        else:
            x_out = dot(jnp.concatenate([high, low], 1), x_ref[...])
        result.append(x_out[:, :length] + x_out[:, length:] + y_out[:, i * length : (i + 1) * length])
    return result


def z_part(lowers, uppers, z_ref):
    def side_by_side(pieces):
        return jnp.concatenate([p.reshape(-1, p.shape[2]) for p in pieces], axis=1)

    lower, upper = side_by_side(lowers), side_by_side(uppers)
    inputs = [split(lower + upper), split(lower - upper)]
    even, odd = (
        dot(z_ref[2 * i], high) + dot(z_ref[2 * i + 1], high) + dot(z_ref[2 * i], low)
        for i, (high, low) in enumerate(inputs)
    )
    return even + odd, even - odd


def tiles(i):
    return [pl.ds(pl.multiple_of(i * 16 + 8 * j, 8), 8) for j in range(2)]


def cut(out, j, length):
    return out[:, j * length : (j + 1) * length].reshape(-1, 8, length)


def total(vector):
    return jnp.sum(vector, axis=(0, 1), keepdims=True)


def fold(block):
    return jnp.sum(block.reshape(-1, 8, block.shape[-1]), axis=0)


def prepare(code, wave, consts, states, partly, x_ref, y_ref, z_ref):
    depth, width, length = states.shape
    double = code[0, 0] & 1
    x_row = jnp.concatenate([consts[:length], consts[length : 2 * length]], axis=1)
    x_ref[...] = jnp.concatenate([x_row, x_row], axis=0)
    rows, cols = (lax.broadcasted_iota(jnp.int32, (4 * width, 4 * width), d) for d in range(2))
    for i in range(2):
        at = pl.ds(pl.multiple_of(2 * length + (2 * double + i) * width, width), width)
        square = jnp.concatenate([jnp.concatenate([consts[at]] * 2, axis=1)] * 4, axis=0)
        y_ref[i] = jnp.where(rows // width == cols // width, square, jnp.zeros_like(square))
    half = depth // 2
    z_rows = consts[2 * length + 4 * width : 2 * length + 4 * width + half]
    down = lax.broadcasted_iota(jnp.int32, (8 * half, half), 0) // 8 == lax.broadcasted_iota(jnp.int32, (8 * half, half), 1)
    tall = dot(down.astype(jnp.bfloat16), z_rows).astype(jnp.bfloat16)
    source, target = (lax.broadcasted_iota(jnp.int32, (length, 8 * half), d) for d in range(2))
    for i in range(4):
        full = dot(tall, (source == target // 8 + half * i).astype(jnp.bfloat16))
        z_ref[i] = jnp.where((rows & 7) == (cols & 7), full, 0.0).astype(jnp.bfloat16)
    live = lax.broadcasted_iota(jnp.int32, (1, width, length), 1) < (width // 2) * (1 + double)

    def masked(z):
        s = jnp.where(live, wave[pl.ds(z, 8)].astype(jnp.float32), 0.0)
        states[pl.ds(z, 8)] = s
        return s

    xy_pass(masked, partly, 0, depth, x_ref, y_ref, True)


def xy_pass(read, out, start, lines, x_ref, y_ref, exact):
    _, width, length = out.shape

    def step(i, carry):
        z = start + i * 8
        rows = read(z).reshape(2, 4 * width, length)
        lower, upper = xy_part([rows[0], rows[1]], x_ref, y_ref, exact)
        out[pl.ds(z, 4)] = lower.reshape(4, width, length)
        out[pl.ds(z + 4, 4)] = upper.reshape(4, width, length)
        return carry

    lax.fori_loop(0, lines // 8, step, 0)


def kinetics(after, states, partly, x_ref, y_ref, z_ref, once, again):
    depth, width, length = once.shape
    half = depth // 2

    def z_pass(source, before, out):
        def zz(i, carry):
            halves = [[source[pl.ds(j * half, half), r] for r in tiles(i)] for j in range(2)]
            for j, part in enumerate(z_part(*halves, z_ref)):
                for k, r in enumerate(tiles(i)):
                    at = pl.ds(j * half, half)
                    out[at, r] = before[at, r] + cut(part, k, length)
            return carry

        lax.fori_loop(0, width // 16, zz, 0)

    z_pass(states, partly, once)
    xy_pass(lambda z: once[pl.ds(z, 8)], again, 0, depth, x_ref, y_ref, False)
    z_pass(once, again, again)


def box_rows(band, code, column):
    at, _ = place(band[0] & 1, code[0, 0])
    return [pl.ds(pl.multiple_of(i * column, column), column) for i in (at, 1 - at)]


CHUNKS = ((0, 0), (0, 1), (0, 3), (1, 0), (1, 1), (1, 3), (0, 2), (1, 2))


def chunk_loop(band, code, columns, half, use):
    chip = band[0] >> 1
    for ref, rows in zip(columns, box_rows(band, code, columns[0].shape[2])):
        chunk = ref.shape[1]
        for m, (slab, back) in enumerate(CHUNKS):
            use(pl.ds(slab * half + ((chip - back) & (CHIPS - 1)) * chunk, chunk), rows, ref[m])


def both_steps(band, code, states, kinetic, again, x_ref, y_ref, z_ref, own, other, *refs):
    (keep0, give0, keep1, give1), (pot, forced, total_h, extra, twice) = refs[:4], refs[4:]
    depth, width, length = pot.shape
    half, column, double = depth // 2, width // 2, code[0, 0] & 1
    chunk = half // CHIPS

    def use(lines, rows, v):
        pot[lines, rows] = v
        forced[lines, rows] = v * states[lines, rows]

    chunk_loop(band, code, (own, other), half, use)
    xy_pass(lambda z: forced[pl.ds(z, 8)], extra, 0, depth, x_ref, y_ref, False)

    def zz(i, sums):
        places = [pl.ds(0, half), pl.ds(half, half)]
        parts = z_part(*[[forced[at, r] for r in tiles(i)] for at in places], z_ref)
        for k, r in enumerate(tiles(i)):
            pairs = []
            for at, part in zip(places, parts):
                s, h = states[at, r], kinetic[at, r] + forced[at, r]
                w = again[at, r] + extra[at, r] + cut(part, k, length) + pot[at, r] * h
                total_h[at, r] = h
                twice[at, r] = w
                pairs.append((s * s, s * h, h * h, s * w, h * w, w * w))
            sums = tuple(v + fold(a + b) for v, a, b in zip(sums, *pairs))
        return sums

    zero = jnp.zeros((8, length), jnp.float32)
    ss, sh, hh, sw, hw, ww = (total(v) for v in lax.fori_loop(0, width // 16, zz, (zero,) * 6))
    cells = (2 * half * column * length * (1 + double)).astype(jnp.float32)
    first = 1.0 + STEP_LENGTH * sh / (ss + EPSILON)
    tt = first * first * ss - 2.0 * STEP_LENGTH * first * sh + STEP_LENGTH * STEP_LENGTH * hh
    th = first * first * sh - STEP_LENGTH * first * (hh + sw) + STEP_LENGTH * STEP_LENGTH * hw
    hh = first * first * hh - 2.0 * STEP_LENGTH * first * hw + STEP_LENGTH * STEP_LENGTH * ww
    square = cells / (tt + EPSILON)
    second = 1.0 + STEP_LENGTH * square * th / (square * tt + EPSILON)
    weight = second * second * tt - 2.0 * STEP_LENGTH * second * th + STEP_LENGTH * STEP_LENGTH * hh
    sign = (2 * double - 1).astype(jnp.float32)
    factor = sign / 8.0 * square * cells / (square * weight + EPSILON)
    factor = factor.reshape(1, 1, 1)
    by_s, by_h = ((second * first).reshape(1, 1, 1), (-STEP_LENGTH * (first + second)).reshape(1, 1, 1))
    by_w = STEP_LENGTH * STEP_LENGTH
    for slab, outs in ((1, (keep1, give1)), (0, (keep0, give0))):
        for out, rows in zip(outs, box_rows(band, code, column)):
            for k in range(CHIPS):
                at = pl.ds(slab * half + (((band[0] >> 1) + k) & (CHIPS - 1)) * chunk, chunk)
                u = by_s * states[at, rows] + by_h * total_h[at, rows] + by_w * twice[at, rows]
                out[k] = factor * (u * u)


def stack(after, *refs):
    out, at = refs[-1], 0
    for block in refs[:-1]:
        parts = [block[...]] if len(block.shape) < len(out.shape) else [block[i] for i in range(block.shape[0])]
        for part in parts:
            out[at] = part
            at += 1


def to_next_chip(block, k):
    m = 2 * CHIPS
    return lax.ppermute(block, "band", [(b, (b + 2 * k) % m) for b in range(m)])


def around(blocks):
    sent = {k: to_next_chip(blocks[k], k) for k in ORDER}
    return [blocks[0]] + [sent[k] for k in range(1, CHIPS)]


def to_other_core(block):
    return lax.ppermute(block, "band", [(b, b ^ 1) for b in range(2 * CHIPS)])


def to_group(block, distance):
    n = lax.axis_size("frag")
    return lax.ppermute(block, "frag", [(i, (i + distance) % n) for i in range(n)])


def place(core, code):
    low = code >> 2
    upper = (low + core) & 1
    return upper, ((low + upper) & (2 * CHIPS - 1)) >> 1


def cut_chunks(band, potential, *outs):
    for k, out in enumerate(outs):
        at = (((band[0] >> 1) + k) & (CHIPS - 1)) * out.shape[0]
        out[...] = potential[pl.ds(at, out.shape[0])]


def pick(band, code, code_before, after, *refs):
    for out, order in zip(refs[CHIPS:], (code_before, code)):
        _, owner = place(band[0] & 1, order[0, 0])
        source = ((band[0] >> 1) - owner) & (CHIPS - 1)
        for k in range(CHIPS):

            @pl.when(source == k)
            def _(k=k, out=out):
                out[...] = refs[k][...]


def settle(band, *refs):
    for k, block in enumerate(refs[:CHIPS]):
        chip = ((band[0] >> 1) - k) & (CHIPS - 1)
        refs[CHIPS][pl.ds(chip * block.shape[0], block.shape[0])] = block[...]


def body(wave_init, potential, fragment_order):
    _, _, depth, width, length = wave_init.shape
    chunk, column = depth // 2 // CHIPS, width // 2
    wave = wave_init[0, 0]
    band = lax.axis_index("band").astype(jnp.int32)
    core = band & 1
    order_before = to_group(fragment_order, 1)

    small = pltpu.CompilerParams(vmem_limit_bytes=4 * 1024 * 1024)
    piece, quarter, box = (
        jax.ShapeDtypeStruct(shape + (length,), jnp.float32)
        for shape in ((chunk, column), (CHIPS, chunk, column), (depth, width))
    )
    square = (4 * width, 4 * width)
    ops = [jax.ShapeDtypeStruct(lead + square, jnp.bfloat16) for lead in ((), (2,), (4,))]

    def kernel(function, outs, spaces, params, scratch=(), flops=0):
        return pl.pallas_call(
            function,
            out_shape=outs,
            in_specs=spaces,
            out_specs=[VMEM] * len(outs),
            scratch_shapes=[pltpu.VMEM(a.shape, a.dtype) for a in scratch],
            compiler_params=params,
            cost_estimate=pl.CostEstimate(flops=flops, bytes_accessed=4_000_000, transcendentals=0) if flops else None,
            name=function.__name__,
        )

    pieces = around(kernel(cut_chunks, [piece] * CHIPS, [SMEM, VMEM], small)(band[None], potential))
    states, partly, *ops = kernel(prepare, [box] * 2 + ops, [SMEM, VMEM, VMEM], MIDDLE)(
        fragment_order, wave, operators(depth, width, length)
    )
    below, here = kernel(pick, [piece] * 2, [SMEM] * 3 + [ANY] + [VMEM] * CHIPS, small)(
        band[None], fragment_order, order_before, states, *pieces
    )
    below = to_group(below, -1)

    def stacked(after, *blocks):
        count = sum(1 if block.ndim == 3 else block.shape[0] for block in blocks)
        out = jax.ShapeDtypeStruct((count, chunk, column, length), jnp.float32)
        return kernel(stack, [out], [ANY] + [VMEM] * len(blocks), small)(after, *blocks)[0]

    near = [here] + [to_next_chip(here, k) for k in (1, 3)]
    both = stacked(states, here, below)
    far = [below] + [to_next_chip(below, k) for k in (1, 3)] + [to_next_chip(both, 2)]
    kinetic, again = kernel(kinetics, [box] * 2, [ANY] + [VMEM] * 5, MIDDLE, flops=4_000_000_000)(
        both, states, partly, *ops
    )
    own = stacked(again, *near, *far)
    keep0, give0, keep1, give1 = kernel(
        both_steps, [quarter] * 4, [SMEM] * 2 + [VMEM] * 8, BIG, scratch=[box] * 5
    )(band[None], fragment_order, states, kinetic, again, *ops, own, to_other_core(own))

    def reduce_chip(keep, give):
        result, *arrived = around(list(keep + to_other_core(give)))
        for block in arrived:
            result = result + block
        return result

    above = to_group(reduce_chip(keep1, give1), 1)
    here = reduce_chip(keep0, give0)
    owner, owner_before = (place(core, code[0, 0])[1] for code in (fragment_order, order_before))
    sends = []
    for k in range(CHIPS):
        target = ((band >> 1) + k) & (CHIPS - 1)
        sends.append(jnp.where(target == owner, here, 0.0) + jnp.where(target == owner_before, above, 0.0))
    return pl.pallas_call(
        settle,
        out_shape=jax.ShapeDtypeStruct(potential.shape, jnp.float32),
        in_specs=[SMEM] + [VMEM] * CHIPS,
        out_specs=VMEM,
        compiler_params=small,
        name="settle",
    )(band[None], *around(sends))


def solution(mesh):
    placed = (P("frag", "band", None, None, None), P("frag", "band", None), P("frag", None))
    return jax.shard_map(
        body, mesh=mesh, in_specs=placed, out_specs=P("frag", "band", None), check_vma=False
    )
```

```python
import jax
import jax.numpy as jnp
import numpy as np
from jax import lax
from jax.experimental import pallas as pl
from jax.experimental.pallas import tpu as pltpu
from jax.sharding import PartitionSpec as P

STEP_LENGTH = 0.1
EPSILON = 1e-06
CHIPS = 4
ORDER = (1, 3, 2)
VMEM = pl.BlockSpec(memory_space=pltpu.VMEM)
ANY = pl.BlockSpec(memory_space=pl.ANY)
SMEM = pl.BlockSpec(memory_space=pltpu.SMEM)
MIDDLE = pltpu.CompilerParams(vmem_limit_bytes=16 * 1024 * 1024)
BIG = pltpu.CompilerParams(vmem_limit_bytes=24 * 1024 * 1024)


def half_kinetic(extent, length):
    m = np.arange(length)
    weight = (2.0 * np.pi * np.minimum(m, length - m) / length) ** 2
    angle = 2.0 * np.pi * (m[:, None] * m[None, :] % length) / length
    matrix = (np.cos(angle) * weight) @ np.cos(angle).T + (np.sin(angle) * weight) @ np.sin(angle).T
    out = np.zeros((extent, extent))
    out[:length, :length] = 0.5 * matrix / length
    return out


def split_const(matrix):
    whole = jnp.asarray(matrix, jnp.float32)
    high = whole.astype(jnp.bfloat16)
    return high, (whole - high.astype(jnp.float32)).astype(jnp.bfloat16)


def operators(depth, width, length):
    y_pair = [half_kinetic(width, width // 2), half_kinetic(width, width)]
    z_op, half = half_kinetic(depth, depth), depth // 2
    z_parts = [(z_op[:half, :half] + sign * z_op[:half, half:]) / 2 for sign in (1, -1)]
    rows = list(split_const(half_kinetic(length, length)))
    for matrix in y_pair:
        rows += [jnp.concatenate([part, part], axis=1) for part in split_const(matrix)]
    rows.append(jnp.concatenate([part for matrix in z_parts for part in split_const(matrix)], axis=1))
    return jnp.concatenate(rows, axis=0)


def split(value):
    high = value.astype(jnp.bfloat16)
    return high, (value - high.astype(jnp.float32)).astype(jnp.bfloat16)


def dot(a, b):
    return jnp.dot(a, b, preferred_element_type=jnp.float32)


def xy_part(blocks, x_ref, y_ref, exact):
    parts = [(b.astype(jnp.bfloat16), None) if exact else split(b) for b in blocks]
    y_high, y_low = y_ref[0], y_ref[1]
    highs = jnp.concatenate([p[0] for p in parts], axis=1)
    y_out = dot(y_high, highs) + dot(y_low, highs)
    if not exact:
        y_out = y_out + dot(y_high, jnp.concatenate([p[1] for p in parts], axis=1))
    length = blocks[0].shape[1]
    result = []
    for i, (high, low) in enumerate(parts):
        if exact:
            x_out = dot(high, x_ref[:length])
        else:
            x_out = dot(jnp.concatenate([high, low], 1), x_ref[...])
        result.append(x_out[:, :length] + x_out[:, length:] + y_out[:, i * length : (i + 1) * length])
    return result


def z_part(lowers, uppers, z_ref):
    def side_by_side(pieces):
        return jnp.concatenate([p.reshape(-1, p.shape[2]) for p in pieces], axis=1)

    lower, upper = side_by_side(lowers), side_by_side(uppers)
    inputs = [split(lower + upper), split(lower - upper)]
    even, odd = (
        dot(z_ref[2 * i], high) + dot(z_ref[2 * i + 1], high) + dot(z_ref[2 * i], low)
        for i, (high, low) in enumerate(inputs)
    )
    return even + odd, even - odd


def tiles(i):
    return [pl.ds(pl.multiple_of(i * 16 + 8 * j, 8), 8) for j in range(2)]


def cut(out, j, length):
    return out[:, j * length : (j + 1) * length].reshape(-1, 8, length)


def total(vector):
    return jnp.sum(vector, axis=(0, 1), keepdims=True)


def fold(block):
    return jnp.sum(block.reshape(-1, 8, block.shape[-1]), axis=0)


def prepare(code, wave, consts, states, partly, x_ref, y_ref, z_ref):
    depth, width, length = states.shape
    double = code[0, 0] & 1
    x_row = jnp.concatenate([consts[:length], consts[length : 2 * length]], axis=1)
    x_ref[...] = jnp.concatenate([x_row, x_row], axis=0)
    rows, cols = (lax.broadcasted_iota(jnp.int32, (4 * width, 4 * width), d) for d in range(2))
    for i in range(2):
        at = pl.ds(pl.multiple_of(2 * length + (2 * double + i) * width, width), width)
        square = jnp.concatenate([jnp.concatenate([consts[at]] * 2, axis=1)] * 4, axis=0)
        y_ref[i] = jnp.where(rows // width == cols // width, square, jnp.zeros_like(square))
    half = depth // 2
    z_rows = consts[2 * length + 4 * width : 2 * length + 4 * width + half]
    down = lax.broadcasted_iota(jnp.int32, (8 * half, half), 0) // 8 == lax.broadcasted_iota(jnp.int32, (8 * half, half), 1)
    tall = dot(down.astype(jnp.bfloat16), z_rows).astype(jnp.bfloat16)
    source, target = (lax.broadcasted_iota(jnp.int32, (length, 8 * half), d) for d in range(2))
    for i in range(4):
        full = dot(tall, (source == target // 8 + half * i).astype(jnp.bfloat16))
        z_ref[i] = jnp.where((rows & 7) == (cols & 7), full, 0.0).astype(jnp.bfloat16)
    live = lax.broadcasted_iota(jnp.int32, (1, width, length), 1) < (width // 2) * (1 + double)

    def masked(z):
        s = jnp.where(live, wave[pl.ds(z, 8)].astype(jnp.float32), 0.0)
        states[pl.ds(z, 8)] = s
        return s

    xy_pass(masked, partly, 0, depth, x_ref, y_ref, True)


def xy_pass(read, out, start, lines, x_ref, y_ref, exact):
    _, width, length = out.shape

    def step(i, carry):
        z = start + i * 8
        rows = read(z).reshape(2, 4 * width, length)
        lower, upper = xy_part([rows[0], rows[1]], x_ref, y_ref, exact)
        out[pl.ds(z, 4)] = lower.reshape(4, width, length)
        out[pl.ds(z + 4, 4)] = upper.reshape(4, width, length)
        return carry

    lax.fori_loop(0, lines // 8, step, 0)


def kinetics(after, states, partly, z_ref, out):
    depth, width, length = out.shape
    half = depth // 2

    def zz(i, carry):
        halves = [[states[pl.ds(j * half, half), r] for r in tiles(i)] for j in range(2)]
        for j, part in enumerate(z_part(*halves, z_ref)):
            for k, r in enumerate(tiles(i)):
                at = pl.ds(j * half, half)
                out[at, r] = partly[at, r] + cut(part, k, length)
        return carry

    lax.fori_loop(0, width // 16, zz, 0)


def box_rows(band, code, column):
    at, _ = place(band[0] & 1, code[0, 0])
    return [pl.ds(pl.multiple_of(i * column, column), column) for i in (at, 1 - at)]


CHUNKS = ((0, 0), (0, 1), (0, 3), (1, 0), (1, 1), (1, 3), (0, 2), (1, 2))


def chunk_loop(band, code, columns, half, use):
    chip = band[0] >> 1
    for ref, rows in zip(columns, box_rows(band, code, columns[0].shape[2])):
        chunk = ref.shape[1]
        for m, (slab, back) in enumerate(CHUNKS):
            use(pl.ds(slab * half + ((chip - back) & (CHIPS - 1)) * chunk, chunk), rows, ref[m])


def both_steps(band, code, states, kinetic, x_ref, y_ref, z_ref, own, other, *refs):
    (keep0, give0, keep1, give1), (pot, once, extra, twice) = refs[:4], refs[4:]
    depth, width, length = pot.shape
    half, column, double = depth // 2, width // 2, code[0, 0] & 1
    chunk = half // CHIPS

    def use(lines, rows, v):
        pot[lines, rows] = v
        once[lines, rows] = kinetic[lines, rows] + v * states[lines, rows]

    chunk_loop(band, code, (own, other), half, use)
    xy_pass(lambda z: once[pl.ds(z, 8)], extra, 0, depth, x_ref, y_ref, False)

    def zz(i, sums):
        places = [pl.ds(0, half), pl.ds(half, half)]
        parts = z_part(*[[once[at, r] for r in tiles(i)] for at in places], z_ref)
        for k, r in enumerate(tiles(i)):
            pairs = []
            for at, part in zip(places, parts):
                s, h = states[at, r], once[at, r]
                w = extra[at, r] + cut(part, k, length) + pot[at, r] * h
                twice[at, r] = w
                pairs.append((s * s, s * h, h * h, s * w, h * w, w * w))
            sums = tuple(v + fold(a + b) for v, a, b in zip(sums, *pairs))
        return sums

    zero = jnp.zeros((8, length), jnp.float32)
    ss, sh, hh, sw, hw, ww = (total(v) for v in lax.fori_loop(0, width // 16, zz, (zero,) * 6))
    cells = (2 * half * column * length * (1 + double)).astype(jnp.float32)
    first = 1.0 + STEP_LENGTH * sh / (ss + EPSILON)
    tt = first * first * ss - 2.0 * STEP_LENGTH * first * sh + STEP_LENGTH * STEP_LENGTH * hh
    th = first * first * sh - STEP_LENGTH * first * (hh + sw) + STEP_LENGTH * STEP_LENGTH * hw
    hh = first * first * hh - 2.0 * STEP_LENGTH * first * hw + STEP_LENGTH * STEP_LENGTH * ww
    square = cells / (tt + EPSILON)
    second = 1.0 + STEP_LENGTH * square * th / (square * tt + EPSILON)
    weight = second * second * tt - 2.0 * STEP_LENGTH * second * th + STEP_LENGTH * STEP_LENGTH * hh
    sign = (2 * double - 1).astype(jnp.float32)
    factor = sign / 8.0 * square * cells / (square * weight + EPSILON)
    factor = factor.reshape(1, 1, 1)
    by_s, by_h = ((second * first).reshape(1, 1, 1), (-STEP_LENGTH * (first + second)).reshape(1, 1, 1))
    by_w = STEP_LENGTH * STEP_LENGTH
    for slab, outs in ((1, (keep1, give1)), (0, (keep0, give0))):
        for out, rows in zip(outs, box_rows(band, code, column)):
            for k in range(CHIPS):
                at = pl.ds(slab * half + (((band[0] >> 1) + k) & (CHIPS - 1)) * chunk, chunk)
                u = by_s * states[at, rows] + by_h * once[at, rows] + by_w * twice[at, rows]
                out[k] = factor * (u * u)


def stack(after, *refs):
    out, at = refs[-1], 0
    for block in refs[:-1]:
        parts = [block[...]] if len(block.shape) < len(out.shape) else [block[i] for i in range(block.shape[0])]
        for part in parts:
            out[at] = part
            at += 1


def to_next_chip(block, k):
    m = 2 * CHIPS
    return lax.ppermute(block, "band", [(b, (b + 2 * k) % m) for b in range(m)])


def around(blocks):
    sent = {k: to_next_chip(blocks[k], k) for k in ORDER}
    return [blocks[0]] + [sent[k] for k in range(1, CHIPS)]


def to_other_core(block):
    return lax.ppermute(block, "band", [(b, b ^ 1) for b in range(2 * CHIPS)])


def to_group(block, distance):
    n = lax.axis_size("frag")
    return lax.ppermute(block, "frag", [(i, (i + distance) % n) for i in range(n)])


def place(core, code):
    low = code >> 2
    upper = (low + core) & 1
    return upper, ((low + upper) & (2 * CHIPS - 1)) >> 1


def cut_chunks(band, potential, *outs):
    for k, out in enumerate(outs):
        at = (((band[0] >> 1) + k) & (CHIPS - 1)) * out.shape[0]
        out[...] = potential[pl.ds(at, out.shape[0])]


def pick(band, code, code_before, after, *refs):
    for out, order in zip(refs[CHIPS:], (code_before, code)):
        _, owner = place(band[0] & 1, order[0, 0])
        source = ((band[0] >> 1) - owner) & (CHIPS - 1)
        for k in range(CHIPS):

            @pl.when(source == k)
            def _(k=k, out=out):
                out[...] = refs[k][...]


def settle(band, *refs):
    for k, block in enumerate(refs[:CHIPS]):
        chip = ((band[0] >> 1) - k) & (CHIPS - 1)
        refs[CHIPS][pl.ds(chip * block.shape[0], block.shape[0])] = block[...]


def body(wave_init, potential, fragment_order):
    _, _, depth, width, length = wave_init.shape
    chunk, column = depth // 2 // CHIPS, width // 2
    wave = wave_init[0, 0]
    band = lax.axis_index("band").astype(jnp.int32)
    core = band & 1
    order_before = to_group(fragment_order, 1)

    small = pltpu.CompilerParams(vmem_limit_bytes=4 * 1024 * 1024)
    piece, quarter, box = (
        jax.ShapeDtypeStruct(shape + (length,), jnp.float32)
        for shape in ((chunk, column), (CHIPS, chunk, column), (depth, width))
    )
    square = (4 * width, 4 * width)
    ops = [jax.ShapeDtypeStruct(lead + square, jnp.bfloat16) for lead in ((), (2,), (4,))]

    def kernel(function, outs, spaces, params, scratch=(), flops=0):
        return pl.pallas_call(
            function,
            out_shape=outs,
            in_specs=spaces,
            out_specs=[VMEM] * len(outs),
            scratch_shapes=[pltpu.VMEM(a.shape, a.dtype) for a in scratch],
            compiler_params=params,
            cost_estimate=pl.CostEstimate(flops=flops, bytes_accessed=4_000_000, transcendentals=0) if flops else None,
            name=function.__name__,
        )

    pieces = around(kernel(cut_chunks, [piece] * CHIPS, [SMEM, VMEM], small)(band[None], potential))
    states, partly, *ops = kernel(prepare, [box] * 2 + ops, [SMEM, VMEM, VMEM], MIDDLE)(
        fragment_order, wave, operators(depth, width, length)
    )
    below, here = kernel(pick, [piece] * 2, [SMEM] * 3 + [ANY] + [VMEM] * CHIPS, small)(
        band[None], fragment_order, order_before, states, *pieces
    )
    below = to_group(below, -1)

    def stacked(after, *blocks):
        count = sum(1 if block.ndim == 3 else block.shape[0] for block in blocks)
        out = jax.ShapeDtypeStruct((count, chunk, column, length), jnp.float32)
        return kernel(stack, [out], [ANY] + [VMEM] * len(blocks), small)(after, *blocks)[0]

    near = [here] + [to_next_chip(here, k) for k in (1, 3)]
    both = stacked(states, here, below)
    far = [below] + [to_next_chip(below, k) for k in (1, 3)] + [to_next_chip(both, 2)]
    (kinetic,) = kernel(kinetics, [box], [ANY] + [VMEM] * 3, MIDDLE, flops=4_000_000_000)(both, states, partly, ops[2])
    own = stacked(kinetic, *near, *far)
    keep0, give0, keep1, give1 = kernel(
        both_steps, [quarter] * 4, [SMEM] * 2 + [VMEM] * 7, BIG, scratch=[box] * 4
    )(band[None], fragment_order, states, kinetic, *ops, own, to_other_core(own))

    def reduce_chip(keep, give):
        result, *arrived = around(list(keep + to_other_core(give)))
        for block in arrived:
            result = result + block
        return result

    above = to_group(reduce_chip(keep1, give1), 1)
    here = reduce_chip(keep0, give0)
    owner, owner_before = (place(core, code[0, 0])[1] for code in (fragment_order, order_before))
    sends = []
    for k in range(CHIPS):
        target = ((band >> 1) + k) & (CHIPS - 1)
        sends.append(jnp.where(target == owner, here, 0.0) + jnp.where(target == owner_before, above, 0.0))
    return pl.pallas_call(
        settle,
        out_shape=jax.ShapeDtypeStruct(potential.shape, jnp.float32),
        in_specs=[SMEM] + [VMEM] * CHIPS,
        out_specs=VMEM,
        compiler_params=small,
        name="settle",
    )(band[None], *around(sends))


def solution(mesh):
    placed = (P("frag", "band", None, None, None), P("frag", "band", None), P("frag", None))
    return jax.shard_map(
        body, mesh=mesh, in_specs=placed, out_specs=P("frag", "band", None), check_vma=False
    )
```

```python
import jax
import jax.numpy as jnp
import numpy as np
from jax import lax
from jax.experimental import pallas as pl
from jax.experimental.pallas import tpu as pltpu
from jax.sharding import PartitionSpec as P

STEP_LENGTH = 0.1
EPSILON = 1e-06
CHIPS = 4
ORDER = (1, 3, 2)
VMEM = pl.BlockSpec(memory_space=pltpu.VMEM)
ANY = pl.BlockSpec(memory_space=pl.ANY)
SMEM = pl.BlockSpec(memory_space=pltpu.SMEM)
MIDDLE = pltpu.CompilerParams(vmem_limit_bytes=16 * 1024 * 1024)
BIG = pltpu.CompilerParams(vmem_limit_bytes=24 * 1024 * 1024)


def half_kinetic(extent, length):
    m = np.arange(length)
    weight = (2.0 * np.pi * np.minimum(m, length - m) / length) ** 2
    angle = 2.0 * np.pi * (m[:, None] * m[None, :] % length) / length
    matrix = (np.cos(angle) * weight) @ np.cos(angle).T + (np.sin(angle) * weight) @ np.sin(angle).T
    out = np.zeros((extent, extent))
    out[:length, :length] = 0.5 * matrix / length
    return out


def split_const(matrix):
    whole = jnp.asarray(matrix, jnp.float32)
    high = whole.astype(jnp.bfloat16)
    return high, (whole - high.astype(jnp.float32)).astype(jnp.bfloat16)


def operators(depth, width, length):
    y_pair = [half_kinetic(width, width // 2), half_kinetic(width, width)]
    z_op, half = half_kinetic(depth, depth), depth // 2
    z_parts = [(z_op[:half, :half] + sign * z_op[:half, half:]) / 2 for sign in (1, -1)]
    rows = list(split_const(half_kinetic(length, length)))
    for matrix in y_pair:
        rows += [jnp.concatenate([part, part], axis=1) for part in split_const(matrix)]
    rows.append(jnp.concatenate([part for matrix in z_parts for part in split_const(matrix)], axis=1))
    return jnp.concatenate(rows, axis=0)


def split(value):
    high = value.astype(jnp.bfloat16)
    return high, (value - high.astype(jnp.float32)).astype(jnp.bfloat16)


def dot(a, b):
    return jnp.dot(a, b, preferred_element_type=jnp.float32)


def xy_part(blocks, x_ref, y_ref, exact):
    parts = [(b.astype(jnp.bfloat16), None) if exact else split(b) for b in blocks]
    y_high, y_low = y_ref[0], y_ref[1]
    highs = jnp.concatenate([p[0] for p in parts], axis=1)
    y_out = dot(y_high, highs) + dot(y_low, highs)
    if not exact:
        y_out = y_out + dot(y_high, jnp.concatenate([p[1] for p in parts], axis=1))
    length = blocks[0].shape[1]
    result = []
    for i, (high, low) in enumerate(parts):
        if exact:
            x_out = dot(high, x_ref[:length])
        else:
            x_out = dot(jnp.concatenate([high, low], 1), x_ref[...])
        result.append(x_out[:, :length] + x_out[:, length:] + y_out[:, i * length : (i + 1) * length])
    return result


def z_part(lowers, uppers, z_ref):
    def side_by_side(pieces):
        return jnp.concatenate([p.reshape(-1, p.shape[2]) for p in pieces], axis=1)

    lower, upper = side_by_side(lowers), side_by_side(uppers)
    inputs = [split(lower + upper), split(lower - upper)]
    even, odd = (
        dot(z_ref[2 * i], high) + dot(z_ref[2 * i + 1], high) + dot(z_ref[2 * i], low)
        for i, (high, low) in enumerate(inputs)
    )
    return even + odd, even - odd


def tiles(i):
    return [pl.ds(pl.multiple_of(i * 16 + 8 * j, 8), 8) for j in range(2)]


def cut(out, j, length):
    return out[:, j * length : (j + 1) * length].reshape(-1, 8, length)


def total(vector):
    return jnp.sum(vector, axis=(0, 1), keepdims=True)


def fold(block):
    return jnp.sum(block.reshape(-1, 8, block.shape[-1]), axis=0)


def prepare(code, wave, consts, states, partly, x_ref, y_ref, z_ref):
    depth, width, length = states.shape
    double = code[0, 0] & 1
    x_row = jnp.concatenate([consts[:length], consts[length : 2 * length]], axis=1)
    x_ref[...] = jnp.concatenate([x_row, x_row], axis=0)
    rows, cols = (lax.broadcasted_iota(jnp.int32, (4 * width, 4 * width), d) for d in range(2))
    for i in range(2):
        at = pl.ds(pl.multiple_of(2 * length + (2 * double + i) * width, width), width)
        square = jnp.concatenate([jnp.concatenate([consts[at]] * 2, axis=1)] * 4, axis=0)
        y_ref[i] = jnp.where(rows // width == cols // width, square, jnp.zeros_like(square))
    half = depth // 2
    z_rows = consts[2 * length + 4 * width : 2 * length + 4 * width + half]
    down = lax.broadcasted_iota(jnp.int32, (8 * half, half), 0) // 8 == lax.broadcasted_iota(jnp.int32, (8 * half, half), 1)
    tall = dot(down.astype(jnp.bfloat16), z_rows).astype(jnp.bfloat16)
    source, target = (lax.broadcasted_iota(jnp.int32, (length, 8 * half), d) for d in range(2))
    for i in range(4):
        full = dot(tall, (source == target // 8 + half * i).astype(jnp.bfloat16))
        z_ref[i] = jnp.where((rows & 7) == (cols & 7), full, 0.0).astype(jnp.bfloat16)
    live = lax.broadcasted_iota(jnp.int32, (1, width, length), 1) < (width // 2) * (1 + double)

    def masked(z):
        s = jnp.where(live, wave[pl.ds(z, 8)].astype(jnp.float32), 0.0)
        states[pl.ds(z, 8)] = s
        return s

    xy_pass(masked, partly, 0, depth, x_ref, y_ref, True)


def xy_pass(read, out, start, lines, x_ref, y_ref, exact):
    _, width, length = out.shape

    def step(i, carry):
        z = start + i * 8
        rows = read(z).reshape(2, 4 * width, length)
        lower, upper = xy_part([rows[0], rows[1]], x_ref, y_ref, exact)
        out[pl.ds(z, 4)] = lower.reshape(4, width, length)
        out[pl.ds(z + 4, 4)] = upper.reshape(4, width, length)
        return carry

    lax.fori_loop(0, lines // 8, step, 0, unroll=2)


def kinetics(after, states, partly, z_ref, out):
    depth, width, length = out.shape
    half = depth // 2

    def zz(i, carry):
        halves = [[states[pl.ds(j * half, half), r] for r in tiles(i)] for j in range(2)]
        for j, part in enumerate(z_part(*halves, z_ref)):
            for k, r in enumerate(tiles(i)):
                at = pl.ds(j * half, half)
                out[at, r] = partly[at, r] + cut(part, k, length)
        return carry

    lax.fori_loop(0, width // 16, zz, 0)


def box_rows(band, code, column):
    at, _ = place(band[0] & 1, code[0, 0])
    return [pl.ds(pl.multiple_of(i * column, column), column) for i in (at, 1 - at)]


CHUNKS = ((0, 0), (0, 1), (0, 3), (1, 0), (1, 1), (1, 3), (0, 2), (1, 2))


def chunk_loop(band, code, columns, half, use):
    chip = band[0] >> 1
    for ref, rows in zip(columns, box_rows(band, code, columns[0].shape[2])):
        chunk = ref.shape[1]
        for m, (slab, back) in enumerate(CHUNKS):
            use(pl.ds(slab * half + ((chip - back) & (CHIPS - 1)) * chunk, chunk), rows, ref[m])


def both_steps(band, code, states, kinetic, x_ref, y_ref, z_ref, own, other, *refs):
    (keep0, give0, keep1, give1), (pot, once, extra, twice) = refs[:4], refs[4:]
    depth, width, length = pot.shape
    half, column, double = depth // 2, width // 2, code[0, 0] & 1
    chunk = half // CHIPS

    def use(lines, rows, v):
        pot[lines, rows] = v
        once[lines, rows] = kinetic[lines, rows] + v * states[lines, rows]

    chunk_loop(band, code, (own, other), half, use)
    xy_pass(lambda z: once[pl.ds(z, 8)], extra, 0, depth, x_ref, y_ref, False)

    def zz(i, sums):
        places = [pl.ds(0, half), pl.ds(half, half)]
        parts = z_part(*[[once[at, r] for r in tiles(i)] for at in places], z_ref)
        for k, r in enumerate(tiles(i)):
            pairs = []
            for at, part in zip(places, parts):
                s, h = states[at, r], once[at, r]
                w = extra[at, r] + cut(part, k, length) + pot[at, r] * h
                twice[at, r] = w
                pairs.append((s * s, s * h, h * h, s * w, h * w, w * w))
            sums = tuple(v + fold(a + b) for v, a, b in zip(sums, *pairs))
        return sums

    zero = jnp.zeros((8, length), jnp.float32)
    ss, sh, hh, sw, hw, ww = (total(v) for v in lax.fori_loop(0, width // 16, zz, (zero,) * 6, unroll=2))
    cells = (2 * half * column * length * (1 + double)).astype(jnp.float32)
    first = 1.0 + STEP_LENGTH * sh / (ss + EPSILON)
    tt = first * first * ss - 2.0 * STEP_LENGTH * first * sh + STEP_LENGTH * STEP_LENGTH * hh
    th = first * first * sh - STEP_LENGTH * first * (hh + sw) + STEP_LENGTH * STEP_LENGTH * hw
    hh = first * first * hh - 2.0 * STEP_LENGTH * first * hw + STEP_LENGTH * STEP_LENGTH * ww
    square = cells / (tt + EPSILON)
    second = 1.0 + STEP_LENGTH * square * th / (square * tt + EPSILON)
    weight = second * second * tt - 2.0 * STEP_LENGTH * second * th + STEP_LENGTH * STEP_LENGTH * hh
    sign = (2 * double - 1).astype(jnp.float32)
    factor = sign / 8.0 * square * cells / (square * weight + EPSILON)
    factor = factor.reshape(1, 1, 1)
    by_s, by_h = ((second * first).reshape(1, 1, 1), (-STEP_LENGTH * (first + second)).reshape(1, 1, 1))
    by_w = STEP_LENGTH * STEP_LENGTH
    for slab, outs in ((1, (keep1, give1)), (0, (keep0, give0))):
        for out, rows in zip(outs, box_rows(band, code, column)):
            for k in range(CHIPS):
                at = pl.ds(slab * half + (((band[0] >> 1) + k) & (CHIPS - 1)) * chunk, chunk)
                u = by_s * states[at, rows] + by_h * once[at, rows] + by_w * twice[at, rows]
                out[k] = factor * (u * u)


def stack(after, *refs):
    out, at = refs[-1], 0
    for block in refs[:-1]:
        parts = [block[...]] if len(block.shape) < len(out.shape) else [block[i] for i in range(block.shape[0])]
        for part in parts:
            out[at] = part
            at += 1


def to_next_chip(block, k):
    m = 2 * CHIPS
    return lax.ppermute(block, "band", [(b, (b + 2 * k) % m) for b in range(m)])


def around(blocks):
    sent = {k: to_next_chip(blocks[k], k) for k in ORDER}
    return [blocks[0]] + [sent[k] for k in range(1, CHIPS)]


def to_other_core(block):
    return lax.ppermute(block, "band", [(b, b ^ 1) for b in range(2 * CHIPS)])


def to_group(block, distance):
    n = lax.axis_size("frag")
    return lax.ppermute(block, "frag", [(i, (i + distance) % n) for i in range(n)])


def place(core, code):
    low = code >> 2
    upper = (low + core) & 1
    return upper, ((low + upper) & (2 * CHIPS - 1)) >> 1


def cut_chunks(band, potential, *outs):
    for k, out in enumerate(outs):
        at = (((band[0] >> 1) + k) & (CHIPS - 1)) * out.shape[0]
        out[...] = potential[pl.ds(at, out.shape[0])]


def pick(band, code, code_before, after, *refs):
    for out, order in zip(refs[CHIPS:], (code_before, code)):
        _, owner = place(band[0] & 1, order[0, 0])
        source = ((band[0] >> 1) - owner) & (CHIPS - 1)
        for k in range(CHIPS):

            @pl.when(source == k)
            def _(k=k, out=out):
                out[...] = refs[k][...]


def settle(band, *refs):
    for k, block in enumerate(refs[:CHIPS]):
        chip = ((band[0] >> 1) - k) & (CHIPS - 1)
        refs[CHIPS][pl.ds(chip * block.shape[0], block.shape[0])] = block[...]


def body(wave_init, potential, fragment_order):
    _, _, depth, width, length = wave_init.shape
    chunk, column = depth // 2 // CHIPS, width // 2
    wave = wave_init[0, 0]
    band = lax.axis_index("band").astype(jnp.int32)
    core = band & 1
    order_before = to_group(fragment_order, 1)

    small = pltpu.CompilerParams(vmem_limit_bytes=4 * 1024 * 1024)
    piece, quarter, box = (
        jax.ShapeDtypeStruct(shape + (length,), jnp.float32)
        for shape in ((chunk, column), (CHIPS, chunk, column), (depth, width))
    )
    square = (4 * width, 4 * width)
    ops = [jax.ShapeDtypeStruct(lead + square, jnp.bfloat16) for lead in ((), (2,), (4,))]

    def kernel(function, outs, spaces, params, scratch=(), flops=0):
        return pl.pallas_call(
            function,
            out_shape=outs,
            in_specs=spaces,
            out_specs=[VMEM] * len(outs),
            scratch_shapes=[pltpu.VMEM(a.shape, a.dtype) for a in scratch],
            compiler_params=params,
            cost_estimate=pl.CostEstimate(flops=flops, bytes_accessed=4_000_000, transcendentals=0) if flops else None,
            name=function.__name__,
        )

    pieces = around(kernel(cut_chunks, [piece] * CHIPS, [SMEM, VMEM], small)(band[None], potential))
    states, partly, *ops = kernel(prepare, [box] * 2 + ops, [SMEM, VMEM, VMEM], MIDDLE)(
        fragment_order, wave, operators(depth, width, length)
    )
    below, here = kernel(pick, [piece] * 2, [SMEM] * 3 + [ANY] + [VMEM] * CHIPS, small)(
        band[None], fragment_order, order_before, states, *pieces
    )
    below = to_group(below, -1)

    def stacked(after, *blocks):
        count = sum(1 if block.ndim == 3 else block.shape[0] for block in blocks)
        out = jax.ShapeDtypeStruct((count, chunk, column, length), jnp.float32)
        return kernel(stack, [out], [ANY] + [VMEM] * len(blocks), small)(after, *blocks)[0]

    near = [here] + [to_next_chip(here, k) for k in (1, 3)]
    both = stacked(states, here, below)
    far = [below] + [to_next_chip(below, k) for k in (1, 3)] + [to_next_chip(both, 2)]
    (kinetic,) = kernel(kinetics, [box], [ANY] + [VMEM] * 3, MIDDLE, flops=4_000_000_000)(both, states, partly, ops[2])
    own = stacked(kinetic, *near, *far)
    keep0, give0, keep1, give1 = kernel(
        both_steps, [quarter] * 4, [SMEM] * 2 + [VMEM] * 7, BIG, scratch=[box] * 4
    )(band[None], fragment_order, states, kinetic, *ops, own, to_other_core(own))

    def reduce_chip(keep, give):
        result, *arrived = around(list(keep + to_other_core(give)))
        for block in arrived:
            result = result + block
        return result

    above = to_group(reduce_chip(keep1, give1), 1)
    here = reduce_chip(keep0, give0)
    owner, owner_before = (place(core, code[0, 0])[1] for code in (fragment_order, order_before))
    sends = []
    for k in range(CHIPS):
        target = ((band >> 1) + k) & (CHIPS - 1)
        sends.append(jnp.where(target == owner, here, 0.0) + jnp.where(target == owner_before, above, 0.0))
    return pl.pallas_call(
        settle,
        out_shape=jax.ShapeDtypeStruct(potential.shape, jnp.float32),
        in_specs=[SMEM] + [VMEM] * CHIPS,
        out_specs=VMEM,
        compiler_params=small,
        name="settle",
    )(band[None], *around(sends))


def solution(mesh):
    placed = (P("frag", "band", None, None, None), P("frag", "band", None), P("frag", None))
    return jax.shard_map(
        body, mesh=mesh, in_specs=placed, out_specs=P("frag", "band", None), check_vma=False
    )
```

```python
import jax
import jax.numpy as jnp
import numpy as np
from jax import lax
from jax.experimental import pallas as pl
from jax.experimental.pallas import tpu as pltpu
from jax.sharding import PartitionSpec as P

STEP_LENGTH = 0.1
EPSILON = 1e-06
CHIPS = 4
ORDER = (1, 3, 2)
VMEM = pl.BlockSpec(memory_space=pltpu.VMEM)
ANY = pl.BlockSpec(memory_space=pl.ANY)
SMEM = pl.BlockSpec(memory_space=pltpu.SMEM)
MIDDLE = pltpu.CompilerParams(vmem_limit_bytes=16 * 1024 * 1024)
BIG = pltpu.CompilerParams(vmem_limit_bytes=24 * 1024 * 1024)


def half_kinetic(extent, length):
    m = np.arange(length)
    weight = (2.0 * np.pi * np.minimum(m, length - m) / length) ** 2
    angle = 2.0 * np.pi * (m[:, None] * m[None, :] % length) / length
    matrix = (np.cos(angle) * weight) @ np.cos(angle).T + (np.sin(angle) * weight) @ np.sin(angle).T
    out = np.zeros((extent, extent))
    out[:length, :length] = 0.5 * matrix / length
    return out


def split_const(matrix):
    whole = jnp.asarray(matrix, jnp.float32)
    high = whole.astype(jnp.bfloat16)
    return high, (whole - high.astype(jnp.float32)).astype(jnp.bfloat16)


def operators(depth, width, length):
    y_pair = [half_kinetic(width, width // 2), half_kinetic(width, width)]
    z_op, half = half_kinetic(depth, depth), depth // 2
    z_parts = [(z_op[:half, :half] + sign * z_op[:half, half:]) / 2 for sign in (1, -1)]
    rows = list(split_const(half_kinetic(length, length)))
    for matrix in y_pair:
        rows += [jnp.concatenate([part, part], axis=1) for part in split_const(matrix)]
    rows.append(jnp.concatenate([part for matrix in z_parts for part in split_const(matrix)], axis=1))
    return jnp.concatenate(rows, axis=0)


def split(value):
    high = value.astype(jnp.bfloat16)
    return high, (value - high.astype(jnp.float32)).astype(jnp.bfloat16)


def dot(a, b):
    return jnp.dot(a, b, preferred_element_type=jnp.float32)


def xy_part(blocks, x_ref, y_ref, exact):
    parts = [(b.astype(jnp.bfloat16), None) if exact else split(b) for b in blocks]
    y_high, y_low = y_ref[0], y_ref[1]
    highs = jnp.concatenate([p[0] for p in parts], axis=1)
    y_out = dot(y_high, highs) + dot(y_low, highs)
    if not exact:
        y_out = y_out + dot(y_high, jnp.concatenate([p[1] for p in parts], axis=1))
    length = blocks[0].shape[1]
    result = []
    for i, (high, low) in enumerate(parts):
        if exact:
            x_out = dot(high, x_ref[:length])
        else:
            x_out = dot(jnp.concatenate([high, low], 1), x_ref[...])
        result.append(x_out[:, :length] + x_out[:, length:] + y_out[:, i * length : (i + 1) * length])
    return result


def z_part(lowers, uppers, z_ref):
    def side_by_side(pieces):
        return jnp.concatenate([p.reshape(-1, p.shape[2]) for p in pieces], axis=1)

    lower, upper = side_by_side(lowers), side_by_side(uppers)
    inputs = [split(lower + upper), split(lower - upper)]
    even, odd = (
        dot(z_ref[2 * i], high) + dot(z_ref[2 * i + 1], high) + dot(z_ref[2 * i], low)
        for i, (high, low) in enumerate(inputs)
    )
    return even + odd, even - odd


def tiles(i):
    return [pl.ds(pl.multiple_of(i * 16 + 8 * j, 8), 8) for j in range(2)]


def cut(out, j, length):
    return out[:, j * length : (j + 1) * length].reshape(-1, 8, length)


def total(vector):
    return jnp.sum(vector, axis=(0, 1), keepdims=True)


def fold(block):
    return jnp.sum(block.reshape(-1, 8, block.shape[-1]), axis=0)


def prepare(code, wave, consts, states, partly, x_ref, y_ref, z_ref):
    depth, width, length = states.shape
    double = code[0, 0] & 1
    x_row = jnp.concatenate([consts[:length], consts[length : 2 * length]], axis=1)
    x_ref[...] = jnp.concatenate([x_row, x_row], axis=0)
    rows, cols = (lax.broadcasted_iota(jnp.int32, (4 * width, 4 * width), d) for d in range(2))
    for i in range(2):
        at = pl.ds(pl.multiple_of(2 * length + (2 * double + i) * width, width), width)
        square = jnp.concatenate([jnp.concatenate([consts[at]] * 2, axis=1)] * 4, axis=0)
        y_ref[i] = jnp.where(rows // width == cols // width, square, jnp.zeros_like(square))
    half = depth // 2
    z_rows = consts[2 * length + 4 * width : 2 * length + 4 * width + half]
    down = lax.broadcasted_iota(jnp.int32, (8 * half, half), 0) // 8 == lax.broadcasted_iota(jnp.int32, (8 * half, half), 1)
    tall = dot(down.astype(jnp.bfloat16), z_rows).astype(jnp.bfloat16)
    source, target = (lax.broadcasted_iota(jnp.int32, (length, 8 * half), d) for d in range(2))
    for i in range(4):
        full = dot(tall, (source == target // 8 + half * i).astype(jnp.bfloat16))
        z_ref[i] = jnp.where((rows & 7) == (cols & 7), full, 0.0).astype(jnp.bfloat16)
    live = lax.broadcasted_iota(jnp.int32, (1, width, length), 1) < (width // 2) * (1 + double)

    def masked(z):
        s = jnp.where(live, wave[pl.ds(z, 8)].astype(jnp.float32), 0.0)
        states[pl.ds(z, 8)] = s
        return s

    xy_pass(masked, partly, 0, depth, x_ref, y_ref, True)


def xy_pass(read, out, start, lines, x_ref, y_ref, exact):
    _, width, length = out.shape

    def step(i, carry):
        z = start + i * 8
        rows = read(z).reshape(2, 4 * width, length)
        lower, upper = xy_part([rows[0], rows[1]], x_ref, y_ref, exact)
        out[pl.ds(z, 4)] = lower.reshape(4, width, length)
        out[pl.ds(z + 4, 4)] = upper.reshape(4, width, length)
        return carry

    lax.fori_loop(0, lines // 8, step, 0, unroll=4)


def kinetics(after, states, partly, z_ref, out):
    depth, width, length = out.shape
    half = depth // 2

    def zz(i, carry):
        halves = [[states[pl.ds(j * half, half), r] for r in tiles(i)] for j in range(2)]
        for j, part in enumerate(z_part(*halves, z_ref)):
            for k, r in enumerate(tiles(i)):
                at = pl.ds(j * half, half)
                out[at, r] = partly[at, r] + cut(part, k, length)
        return carry

    lax.fori_loop(0, width // 16, zz, 0)


def box_rows(band, code, column):
    at, _ = place(band[0] & 1, code[0, 0])
    return [pl.ds(pl.multiple_of(i * column, column), column) for i in (at, 1 - at)]


CHUNKS = ((0, 0), (0, 1), (0, 3), (1, 0), (1, 1), (1, 3), (0, 2), (1, 2))


def chunk_loop(band, code, columns, half, use):
    chip = band[0] >> 1
    for ref, rows in zip(columns, box_rows(band, code, columns[0].shape[2])):
        chunk = ref.shape[1]
        for m, (slab, back) in enumerate(CHUNKS):
            use(pl.ds(slab * half + ((chip - back) & (CHIPS - 1)) * chunk, chunk), rows, ref[m])


def both_steps(band, code, states, kinetic, x_ref, y_ref, z_ref, own, other, *refs):
    (keep0, give0, keep1, give1), (pot, once, extra, twice) = refs[:4], refs[4:]
    depth, width, length = pot.shape
    half, column, double = depth // 2, width // 2, code[0, 0] & 1
    chunk = half // CHIPS

    def use(lines, rows, v):
        pot[lines, rows] = v
        once[lines, rows] = kinetic[lines, rows] + v * states[lines, rows]

    chunk_loop(band, code, (own, other), half, use)
    xy_pass(lambda z: once[pl.ds(z, 8)], extra, 0, depth, x_ref, y_ref, False)

    def zz(i, sums):
        places = [pl.ds(0, half), pl.ds(half, half)]
        parts = z_part(*[[once[at, r] for r in tiles(i)] for at in places], z_ref)
        for k, r in enumerate(tiles(i)):
            pairs = []
            for at, part in zip(places, parts):
                s, h = states[at, r], once[at, r]
                w = extra[at, r] + cut(part, k, length) + pot[at, r] * h
                twice[at, r] = w
                pairs.append((s * s, s * h, h * h, s * w, h * w, w * w))
            sums = tuple(v + fold(a + b) for v, a, b in zip(sums, *pairs))
        return sums

    zero = jnp.zeros((8, length), jnp.float32)
    ss, sh, hh, sw, hw, ww = (total(v) for v in lax.fori_loop(0, width // 16, zz, (zero,) * 6, unroll=4))
    cells = (2 * half * column * length * (1 + double)).astype(jnp.float32)
    first = 1.0 + STEP_LENGTH * sh / (ss + EPSILON)
    tt = first * first * ss - 2.0 * STEP_LENGTH * first * sh + STEP_LENGTH * STEP_LENGTH * hh
    th = first * first * sh - STEP_LENGTH * first * (hh + sw) + STEP_LENGTH * STEP_LENGTH * hw
    hh = first * first * hh - 2.0 * STEP_LENGTH * first * hw + STEP_LENGTH * STEP_LENGTH * ww
    square = cells / (tt + EPSILON)
    second = 1.0 + STEP_LENGTH * square * th / (square * tt + EPSILON)
    weight = second * second * tt - 2.0 * STEP_LENGTH * second * th + STEP_LENGTH * STEP_LENGTH * hh
    sign = (2 * double - 1).astype(jnp.float32)
    factor = sign / 8.0 * square * cells / (square * weight + EPSILON)
    factor = factor.reshape(1, 1, 1)
    by_s, by_h = ((second * first).reshape(1, 1, 1), (-STEP_LENGTH * (first + second)).reshape(1, 1, 1))
    by_w = STEP_LENGTH * STEP_LENGTH
    for slab, outs in ((1, (keep1, give1)), (0, (keep0, give0))):
        for out, rows in zip(outs, box_rows(band, code, column)):
            for k in range(CHIPS):
                at = pl.ds(slab * half + (((band[0] >> 1) + k) & (CHIPS - 1)) * chunk, chunk)
                u = by_s * states[at, rows] + by_h * once[at, rows] + by_w * twice[at, rows]
                out[k] = factor * (u * u)


def stack(after, *refs):
    out, at = refs[-1], 0
    for block in refs[:-1]:
        parts = [block[...]] if len(block.shape) < len(out.shape) else [block[i] for i in range(block.shape[0])]
        for part in parts:
            out[at] = part
            at += 1


def to_next_chip(block, k):
    m = 2 * CHIPS
    return lax.ppermute(block, "band", [(b, (b + 2 * k) % m) for b in range(m)])


def around(blocks):
    sent = {k: to_next_chip(blocks[k], k) for k in ORDER}
    return [blocks[0]] + [sent[k] for k in range(1, CHIPS)]


def to_other_core(block):
    return lax.ppermute(block, "band", [(b, b ^ 1) for b in range(2 * CHIPS)])


def to_group(block, distance):
    n = lax.axis_size("frag")
    return lax.ppermute(block, "frag", [(i, (i + distance) % n) for i in range(n)])


def place(core, code):
    low = code >> 2
    upper = (low + core) & 1
    return upper, ((low + upper) & (2 * CHIPS - 1)) >> 1


def cut_chunks(band, potential, *outs):
    for k, out in enumerate(outs):
        at = (((band[0] >> 1) + k) & (CHIPS - 1)) * out.shape[0]
        out[...] = potential[pl.ds(at, out.shape[0])]


def pick(band, code, code_before, after, *refs):
    for out, order in zip(refs[CHIPS:], (code_before, code)):
        _, owner = place(band[0] & 1, order[0, 0])
        source = ((band[0] >> 1) - owner) & (CHIPS - 1)
        for k in range(CHIPS):

            @pl.when(source == k)
            def _(k=k, out=out):
                out[...] = refs[k][...]


def settle(band, *refs):
    for k, block in enumerate(refs[:CHIPS]):
        chip = ((band[0] >> 1) - k) & (CHIPS - 1)
        refs[CHIPS][pl.ds(chip * block.shape[0], block.shape[0])] = block[...]


def body(wave_init, potential, fragment_order):
    _, _, depth, width, length = wave_init.shape
    chunk, column = depth // 2 // CHIPS, width // 2
    wave = wave_init[0, 0]
    band = lax.axis_index("band").astype(jnp.int32)
    core = band & 1
    order_before = to_group(fragment_order, 1)

    small = pltpu.CompilerParams(vmem_limit_bytes=4 * 1024 * 1024)
    piece, quarter, box = (
        jax.ShapeDtypeStruct(shape + (length,), jnp.float32)
        for shape in ((chunk, column), (CHIPS, chunk, column), (depth, width))
    )
    square = (4 * width, 4 * width)
    ops = [jax.ShapeDtypeStruct(lead + square, jnp.bfloat16) for lead in ((), (2,), (4,))]

    def kernel(function, outs, spaces, params, scratch=(), flops=0):
        return pl.pallas_call(
            function,
            out_shape=outs,
            in_specs=spaces,
            out_specs=[VMEM] * len(outs),
            scratch_shapes=[pltpu.VMEM(a.shape, a.dtype) for a in scratch],
            compiler_params=params,
            cost_estimate=pl.CostEstimate(flops=flops, bytes_accessed=4_000_000, transcendentals=0) if flops else None,
            name=function.__name__,
        )

    pieces = around(kernel(cut_chunks, [piece] * CHIPS, [SMEM, VMEM], small)(band[None], potential))
    states, partly, *ops = kernel(prepare, [box] * 2 + ops, [SMEM, VMEM, VMEM], MIDDLE)(
        fragment_order, wave, operators(depth, width, length)
    )
    below, here = kernel(pick, [piece] * 2, [SMEM] * 3 + [ANY] + [VMEM] * CHIPS, small)(
        band[None], fragment_order, order_before, states, *pieces
    )
    below = to_group(below, -1)

    def stacked(after, *blocks):
        count = sum(1 if block.ndim == 3 else block.shape[0] for block in blocks)
        out = jax.ShapeDtypeStruct((count, chunk, column, length), jnp.float32)
        return kernel(stack, [out], [ANY] + [VMEM] * len(blocks), small)(after, *blocks)[0]

    near = [here] + [to_next_chip(here, k) for k in (1, 3)]
    both = stacked(states, here, below)
    far = [below] + [to_next_chip(below, k) for k in (1, 3)] + [to_next_chip(both, 2)]
    (kinetic,) = kernel(kinetics, [box], [ANY] + [VMEM] * 3, MIDDLE, flops=4_000_000_000)(both, states, partly, ops[2])
    own = stacked(kinetic, *near, *far)
    keep0, give0, keep1, give1 = kernel(
        both_steps, [quarter] * 4, [SMEM] * 2 + [VMEM] * 7, BIG, scratch=[box] * 4
    )(band[None], fragment_order, states, kinetic, *ops, own, to_other_core(own))

    def reduce_chip(keep, give):
        result, *arrived = around(list(keep + to_other_core(give)))
        for block in arrived:
            result = result + block
        return result

    above = to_group(reduce_chip(keep1, give1), 1)
    here = reduce_chip(keep0, give0)
    owner, owner_before = (place(core, code[0, 0])[1] for code in (fragment_order, order_before))
    sends = []
    for k in range(CHIPS):
        target = ((band >> 1) + k) & (CHIPS - 1)
        sends.append(jnp.where(target == owner, here, 0.0) + jnp.where(target == owner_before, above, 0.0))
    return pl.pallas_call(
        settle,
        out_shape=jax.ShapeDtypeStruct(potential.shape, jnp.float32),
        in_specs=[SMEM] + [VMEM] * CHIPS,
        out_specs=VMEM,
        compiler_params=small,
        name="settle",
    )(band[None], *around(sends))


def solution(mesh):
    placed = (P("frag", "band", None, None, None), P("frag", "band", None), P("frag", None))
    return jax.shard_map(
        body, mesh=mesh, in_specs=placed, out_specs=P("frag", "band", None), check_vma=False
    )
```
